128 devices in a mesh: dp: 64 (over y, x, z_lo, core), tensor: 2 (over z_hi).
Axes of the slice: x: 4, y: 4, z: 4 (z_hi: 2, z_lo: 2; z = z_hi * 2 + z_lo), core: 2. Of those that a mesh axis runs over, the one named last changes fastest.
Arguments:
- tokens: bfloat16 [16384, 1152], P('dp'), may hold values from -6 to 6
- cotangent: bfloat16 [16384, 1152], P('dp'), may hold values from -16 to 16
- input_gain: bfloat16 [1152], P('dp'), may hold values from 0.25 to 1.75
- query_weight: bfloat16 [1152, 1024], P('dp', 'tensor'), may hold values from -0.1875 to 0.1875
- key_weight: bfloat16 [1152, 256], P('dp'), may hold values from -0.1875 to 0.1875
- value_weight: bfloat16 [1152, 256], P('dp'), may hold values from -0.1875 to 0.1875
- query_gain: bfloat16 [256], P('dp'), may hold values from 0.25 to 1.75
- key_gain: bfloat16 [256], P('dp'), may hold values from 0.25 to 1.75
- output_weight: bfloat16 [1024, 1152], P('tensor', 'dp'), may hold values from -0.1875 to 0.1875
- attention_gain: bfloat16 [1152], P('dp'), may hold values from 0.25 to 1.75
- feed_gain: bfloat16 [1152], P('dp'), may hold values from 0.25 to 1.75
- gate_weight: bfloat16 [1152, 6912], P('dp', 'tensor'), may hold values from -0.1875 to 0.1875
- up_weight: bfloat16 [1152, 6912], P('dp', 'tensor'), may hold values from -0.1875 to 0.1875
- down_weight: bfloat16 [6912, 1152], P('tensor', 'dp'), may hold values from -0.078125 to 0.078125
- output_gain: bfloat16 [1152], P('dp'), may hold values from 0.25 to 1.75
Outputs:
- layer_out: bfloat16 [16384, 1152], P('dp')
- input_grad: float32 [16384, 1152], P('dp')
- input_gain_grad: float32 [1152], P('dp')
- query_weight_grad: float32 [1152, 1024], P('dp', 'tensor')
- key_weight_grad: float32 [1152, 256], P('dp')
- value_weight_grad: float32 [1152, 256], P('dp')
- query_gain_grad: float32 [256], P('dp')
- key_gain_grad: float32 [256], P('dp')
- output_weight_grad: float32 [1024, 1152], P('tensor', 'dp')
- attention_gain_grad: float32 [1152], P('dp')
- feed_gain_grad: float32 [1152], P('dp')
- gate_weight_grad: float32 [1152, 6912], P('dp', 'tensor')
- up_weight_grad: float32 [1152, 6912], P('dp', 'tensor')
- down_weight_grad: float32 [6912, 1152], P('tensor', 'dp')
- output_gain_grad: float32 [1152], P('dp')
The draws below stay inside these ranges and needn't reach their ends.
All inputs are finite; a program needn't handle non-finite values.
Results may differ from the reference program's by a relative error of at most 0.024.
Values may be sent and summed in bfloat16 or wider, within the bound.
No kernel may reach another device: no remote copies, remote signals or barrier semaphores. Data moves between devices by JAX's collectives and lax.ppermute only.
A program may use at most 320 MiB of HBM per device.

```python
import math
import jax
import jax.numpy as jnp
from jax import lax

D = 1152
NH = 4
HD = 256
FF = 6912
SEQ = 256
TOKENS = 16384
N_DP = 64


def raised(values, stream_key, source, target, blocks, factor):
    owner, partner = [(jnp.arange(values.shape[position]) // (values.shape[position] // blocks)).reshape([-1 if axis == position else 1 for axis in range(values.ndim)]) for position in (source, target)]
    chosen = jax.random.permutation(stream_key, blocks)[partner]
    strong = (owner == chosen) | (owner == (partner + blocks // 2) % blocks)
    return jnp.where(strong, factor * values, values)


def block_levels(key, shape, pieces, low, high):
    def one(dim, parts):
        draws = jax.random.uniform(jax.random.fold_in(jax.random.fold_in(key, 6), dim), (parts,), jnp.float32, low / len(pieces), high / len(pieces))
        return jnp.repeat(jnp.exp(draws), shape[dim] // parts).reshape((-1,) + (1,) * (len(shape) - dim - 1))

    factor_of = one(*pieces[0])
    for cut in pieces[1:]:
        factor_of = factor_of * one(*cut)
    return factor_of


def gaussian(stream_key, dims, spread, reach, cuts=(), held_as=jnp.bfloat16):
    array = spread * jax.random.normal(stream_key, dims, jnp.float32)
    if cuts:
        array = array * block_levels(stream_key, dims, cuts, -0.22, 0.18)
    return jnp.clip(array, -reach, reach).astype(held_as)


def bell_draw_with(stream_key, shape, deviation, reach, cuts, heavy, held_as=jnp.bfloat16):
    drawn = deviation * jax.random.normal(stream_key, shape, jnp.float32)
    if cuts:
        drawn = drawn * block_levels(stream_key, shape, cuts, -0.22, 0.18)
    return jnp.clip(raised(drawn, jax.random.fold_in(stream_key, 3), *heavy), -reach, reach).astype(held_as)


def setup_inputs(seed: int = 0) -> dict:
    seeds = jax.random.split(jax.random.key(seed), 16)
    tokens = gaussian(seeds[0], (TOKENS, D), 1.0, 6.0, ((0, 64),))
    cotangent = bell_draw_with(seeds[1], (TOKENS, D), 1.0, 16.0, ((0, 64),), (0, 1, 64, 4.0))
    input_gain = jnp.clip(1.0 + 0.15 * jax.random.normal(seeds[2], (D,), jnp.float32), 0.25, 1.75).astype(jnp.bfloat16)
    query_weight = gaussian(seeds[3], (D, NH * HD), D ** -0.5, 0.1875, ((0, 64), (1, 2)))
    key_weight = gaussian(seeds[4], (D, HD), D ** -0.5, 0.1875, ((0, 64),))
    value_weight = gaussian(seeds[5], (D, HD), D ** -0.5, 0.1875, ((0, 64),))
    query_gain = jnp.clip(1.0 + 0.15 * jax.random.normal(seeds[6], (HD,), jnp.float32), 0.25, 1.75).astype(jnp.bfloat16)
    key_gain = jnp.clip(1.0 + 0.15 * jax.random.normal(seeds[7], (HD,), jnp.float32), 0.25, 1.75).astype(jnp.bfloat16)
    output_weight = gaussian(seeds[8], (NH * HD, D), (NH * HD) ** -0.5, 0.1875, ((0, 2), (1, 64)))
    attention_gain = jnp.clip(1.0 + 0.15 * jax.random.normal(seeds[9], (D,), jnp.float32), 0.25, 1.75).astype(jnp.bfloat16)
    feed_gain = jnp.clip(1.0 + 0.15 * jax.random.normal(seeds[10], (D,), jnp.float32), 0.25, 1.75).astype(jnp.bfloat16)
    gate_weight = gaussian(seeds[11], (D, FF), D ** -0.5, 0.1875, ((0, 64), (1, 2)))
    up_weight = gaussian(seeds[12], (D, FF), D ** -0.5, 0.1875, ((0, 64), (1, 2)))
    down_weight = gaussian(seeds[13], (FF, D), FF ** -0.5, 0.078125, ((0, 2), (1, 64)))
    output_gain = jnp.clip(1.0 + 0.15 * jax.random.normal(seeds[14], (D,), jnp.float32), 0.25, 1.75).astype(jnp.bfloat16)
    return {"tokens": tokens, "cotangent": cotangent, "input_gain": input_gain, "query_weight": query_weight, "key_weight": key_weight, "value_weight": value_weight, "query_gain": query_gain, "key_gain": key_gain, "output_weight": output_weight, "attention_gain": attention_gain, "feed_gain": feed_gain, "gate_weight": gate_weight, "up_weight": up_weight, "down_weight": down_weight, "output_gain": output_gain}


EPS = 1e-06
THETA = 1000000.0

@jax.custom_vjp
def low(v):
    return lax.optimization_barrier(v.astype(jnp.bfloat16)).astype(jnp.float32)

@jax.custom_vjp
def low_back(v):
    return v

def low_keep(v):
    return (low(v), None)

def low_pass(kept, grad):
    return (grad,)

def back_keep(v):
    return (v, None)

def back_low(kept, grad):
    return (low(grad),)
low.defvjp(low_keep, low_pass)
low_back.defvjp(back_keep, back_low)

def normalize(field, gain):
    return field * lax.rsqrt(lax.optimization_barrier(jnp.mean(field * field, axis=-1, keepdims=True)) + EPS) * gain

def rotate(field):
    length = field.shape[-3]
    half = field.shape[-1] // 2
    freq = THETA ** (-jnp.arange(half, dtype=jnp.float32) / half)
    angle = jnp.arange(length, dtype=jnp.float32)[:, None] * freq[None, :]
    cosine = jnp.cos(angle)[:, None, :]
    sine = jnp.sin(angle)[:, None, :]
    first = field[..., :half]
    second = field[..., half:]
    return jnp.concatenate([first * cosine - second * sine, second * cosine + first * sine], axis=-1)

def product(left, right):
    return jnp.dot(left, right, precision=lax.Precision.HIGHEST, preferred_element_type=jnp.float32)

def attend(block):
    queries, keys, values = block
    scale = queries.shape[-1] ** (-0.5)
    scores = jnp.einsum('qhd,kd->hqk', queries, keys, precision=lax.Precision.HIGHEST) * scale
    scores = low_back(scores)
    length = scores.shape[-1]
    rows = jnp.arange(length)[:, None]
    cols = jnp.arange(length)[None, :]
    scores = jnp.where(cols <= rows, scores, -1e+30)
    weights = low(jax.nn.softmax(scores, axis=-1))
    return jnp.einsum('hqk,kd->qhd', weights, values, precision=lax.Precision.HIGHEST)

def forward_group(rows, input_gain, query_weight, key_weight, value_weight, query_gain, key_gain, output_weight, attention_gain, feed_gain, gate_weight, up_weight, down_weight, output_gain):
    group = rows.shape[0] // SEQ
    normed = low(normalize(rows, input_gain))
    queries = low_back(product(normed, query_weight)).reshape(group, SEQ, NH, HD)
    keys = low_back(product(normed, key_weight)).reshape(group, SEQ, 1, HD)
    values = low(low_back(product(normed, value_weight))).reshape(group, SEQ, HD)
    queries = low(rotate(normalize(queries, query_gain)))
    keys = low(rotate(normalize(keys, key_gain)))[:, :, 0, :]
    mixed = lax.map(jax.checkpoint(attend), (queries, keys, values))
    mixed = low(low_back(mixed)).reshape(rows.shape[0], NH * HD)
    branch = low_back(product(mixed, output_weight))
    hidden_state = rows + normalize(branch, attention_gain)
    feed = low(normalize(hidden_state, feed_gain))
    gate = low_back(product(feed, gate_weight))
    upper = low_back(product(feed, up_weight))
    activ = low(jax.nn.gelu(gate, approximate=True) * upper)
    second = low_back(product(activ, down_weight))
    return hidden_state + normalize(second, output_gain)

def reference(tokens, cotangent, input_gain, query_weight, key_weight, value_weight, query_gain, key_gain, output_weight, attention_gain, feed_gain, gate_weight, up_weight, down_weight, output_gain):
    params = tuple((item.astype(jnp.float32) for item in (input_gain, query_weight, key_weight, value_weight, query_gain, key_gain, output_weight, attention_gain, feed_gain, gate_weight, up_weight, down_weight, output_gain)))
    group = math.gcd(N_DP, max(1, 4096 // SEQ))
    count = N_DP // group
    inputs = tokens.astype(jnp.float32).reshape(count, group * SEQ, D)
    upstream = cotangent.astype(jnp.float32).reshape(count, group * SEQ, D)

    def step(totals, pair):
        block, cot_block = pair
        result, pullback = jax.vjp(forward_group, block, *params)
        grads = pullback(cot_block)
        totals = tuple((first + second for first, second in zip(totals, grads[1:])))
        return (totals, (result, grads[0]))
    start = tuple((jnp.zeros_like(item) for item in params))
    totals, (results, input_grads) = lax.scan(step, start, (inputs, upstream))
    return (results.reshape(TOKENS, D).astype(jnp.bfloat16), input_grads.reshape(TOKENS, D), totals[0], totals[1], totals[2], totals[3], totals[4], totals[5], totals[6], totals[7], totals[8], totals[9], totals[10], totals[11], totals[12])
```

```python
import jax
import jax.numpy as jnp
import numpy as np
from jax import lax
from jax.sharding import Mesh, PartitionSpec as P

D = 1152
HD = 256
SEQ = 256
HALF = SEQ // 2
UNITS = 864
PAD = 896
EPS = 1e-06
THETA = 1000000.0
SCALE = HD ** (-0.5)
BF = jnp.bfloat16
F32 = jnp.float32
PLANE = ("y", "x")


def swap(field, axes, mask, size):
    return lax.ppermute(field, axes, [(i, i ^ mask) for i in range(size)])


def across(field, mask):
    return swap(field, ("zl", "t"), mask, 4)


def other_core(field):
    return swap(field, "c", 1, 2)


def other_member(field):
    return swap(field, "t", 1, 2)


def column_gather(block):
    same = jnp.concatenate([block] + [across(block, m) for m in (1, 2, 3)], axis=0)
    return jnp.concatenate([same, other_core(same)], axis=0)


def column_sum(parts):
    half = parts.shape[0] // 2
    low = parts.astype(BF)
    mine = (low[:half].astype(F32) + other_core(low[half:]).astype(F32)).astype(BF)
    rows = half // 4
    total = mine[:rows].astype(F32)
    for m in (1, 2, 3):
        total = total + across(mine[m * rows : (m + 1) * rows], m).astype(F32)
    return total


def product(left, right):
    return jnp.dot(left, right, preferred_element_type=F32)


def contract_rows(left, right):
    return lax.dot_general(left, right, (((0,), (0,)), ((), ())), preferred_element_type=F32)


def contract_cols(left, right):
    return lax.dot_general(left, right, (((1,), (1,)), ((), ())), preferred_element_type=F32)


def inverse_rms(field):
    return lax.rsqrt(jnp.mean(field * field, axis=-1, keepdims=True) + EPS)


def norm_back(grad, field, inv, gain):
    scaled = grad * gain
    back = inv * scaled - field * (inv * inv * inv) * jnp.mean(field * scaled, axis=-1, keepdims=True)
    return back, grad * field * inv


def tables():
    half = HD // 2
    freq = np.float32(THETA) ** (-np.arange(half, dtype=np.float32) / np.float32(half))
    angle = np.arange(SEQ, dtype=np.float32)[:, None] * freq[None, :].astype(np.float32)
    return jnp.asarray(np.cos(angle).astype(np.float32)), jnp.asarray(np.sin(angle).astype(np.float32))


def rotate(field, cosine, sine):
    half = HD // 2
    first, second = field[..., :half], field[..., half:]
    return jnp.concatenate([first * cosine - second * sine, second * cosine + first * sine], axis=-1)


def quarters(weight):
    cut = weight.reshape(weight.shape[0], 4, UNITS).transpose(1, 0, 2)
    return jnp.pad(cut, ((0, 0), (0, 0), (0, PAD - UNITS)))


def whole_units(block):
    return block[:, :, :UNITS].transpose(1, 0, 2).reshape(block.shape[1], 4 * UNITS)


def on_device(
    tokens,
    cotangent,
    input_gain,
    query_weight,
    key_weight,
    value_weight,
    query_gain,
    key_gain,
    output_weight,
    attention_gain,
    feed_gain,
    gate_weight,
    up_weight,
    down_weight,
    output_gain,
):
    core = lax.axis_index("c")
    member = lax.axis_index("t")
    shard = input_gain.shape[0]
    heads_gain = jnp.concatenate([query_gain, key_gain, jnp.zeros((shard - 8,), BF)])
    gains = jnp.stack([input_gain, attention_gain, feed_gain, output_gain, heads_gain], axis=1)
    gains = jnp.pad(gains, ((0, 0), (0, 123)))
    half0 = jnp.concatenate([query_weight, key_weight, gains], axis=1)
    half1 = jnp.concatenate([value_weight, output_weight.T, gains], axis=1)
    pack = jnp.concatenate(
        [
            jnp.stack([half0, half1, half0, half1]),
            quarters(gate_weight),
            quarters(up_weight),
            quarters(down_weight.T),
        ],
        axis=2,
    )
    got = lax.all_to_all(pack, ("zl", "c"), 0, 0, tiled=True).reshape(4 * shard, -1)
    att_shard = got[:, :PAD]
    att_half = lax.all_to_all(
        jnp.broadcast_to(att_shard[None], (16, *att_shard.shape)), PLANE, 0, 0, tiled=True
    ).reshape(D, PAD)
    feed_weights = lax.all_gather(got[:, PAD:], PLANE, axis=0, tiled=True)

    gain_cols = att_half[:, 768:773].astype(F32).T
    norm_gain, post_gain, feed_scale, final_gain = (gain_cols[i][None, :] for i in range(4))
    head_cols = gain_cols[4].reshape(64, shard)
    query_scale = head_cols[:, :4].reshape(1, HD)
    key_scale = head_cols[:, 4:8].reshape(1, HD)
    own_half = att_half[:, :768]
    their_half = other_core(own_half)
    first_half = jnp.where(core == 0, own_half, their_half)
    second_half = jnp.where(core == 0, their_half, own_half)
    cosine, sine = tables()

    rows = tokens.astype(F32)
    inv_in = inverse_rms(rows)
    normed = (rows * inv_in * norm_gain).astype(BF)
    qk = product(normed, first_half)
    queries = jnp.stack([qk[:, :HD], qk[:, HD : 2 * HD]])
    keys = qk[:, 2 * HD :]
    values = product(normed, second_half[:, :HD]).astype(BF)
    inv_q = inverse_rms(queries)
    inv_k = inverse_rms(keys)
    q_rot = rotate(queries * inv_q * query_scale, cosine, sine).astype(BF)
    k_rot = rotate(keys * inv_k * key_scale, cosine, sine).astype(BF)
    scores = jnp.einsum("hqd,kd->hqk", q_rot, k_rot, preferred_element_type=F32) * SCALE
    causal = jnp.arange(SEQ)[None, :] <= jnp.arange(SEQ)[:, None]
    scores = jnp.where(causal, scores, -1e30)
    expo = jnp.exp(scores - jnp.max(scores, axis=-1, keepdims=True))
    probs_f = expo / jnp.sum(expo, axis=-1, keepdims=True)
    probs = probs_f.astype(BF)
    mixed_heads = jnp.einsum("hqk,kd->hqd", probs, values, preferred_element_type=F32).astype(BF)
    mixed = jnp.concatenate([mixed_heads[0], mixed_heads[1]], axis=1)
    output_t = second_half[:, HD:]
    branch_part = contract_cols(mixed, output_t)

    def my_half(field):
        return lax.dynamic_slice_in_dim(field, member * HALF, HALF, 0)

    def their_rows(field):
        return lax.dynamic_slice_in_dim(field, (1 - member) * HALF, HALF, 0)

    def whole_rows(field):
        theirs = other_member(field)
        top = jnp.where(member == 0, field, theirs)
        bottom = jnp.where(member == 0, theirs, field)
        return jnp.concatenate([top, bottom], axis=0)

    branch = my_half(branch_part) + other_member(their_rows(branch_part).astype(BF)).astype(F32)
    my_rows = my_half(tokens).astype(F32)
    inv_b = inverse_rms(branch)
    hidden = my_rows + branch * inv_b * post_gain
    inv_h = inverse_rms(hidden)
    feed = (hidden * inv_h * feed_scale).astype(BF)

    all_feed = column_gather(feed)
    gate_up = feed_weights[:, : 2 * PAD]
    down_t = feed_weights[:, 2 * PAD :]
    both = product(all_feed, gate_up)
    gate, upper = both[:, :PAD], both[:, PAD:]
    k0 = np.float32(np.sqrt(2.0 / np.pi))
    square = gate * gate
    tanh = jnp.tanh(k0 * gate * (1.0 + 0.044715 * square))
    gelu = 0.5 * gate * (1.0 + tanh)
    slope = 0.5 * (1.0 + tanh) + 0.5 * gate * (1.0 - tanh * tanh) * (k0 * (1.0 + 3 * 0.044715 * square))
    activ = (gelu * upper).astype(BF)
    second = column_sum(contract_cols(activ, down_t))
    inv_s = inverse_rms(second)
    layer_half = (hidden + second * inv_s * final_gain).astype(BF)
    layer_out = whole_rows(layer_half)

    upstream = my_half(cotangent).astype(F32)
    grad_second, final_terms = norm_back(upstream, second, inv_s, final_gain)
    all_grad = column_gather(grad_second.astype(BF))
    grad_activ = product(all_grad, down_t)
    grad_gate = (grad_activ * upper * slope).astype(BF)
    grad_upper = (grad_activ * gelu).astype(BF)
    grad_both = jnp.concatenate([grad_gate, grad_upper], axis=1)
    feed_back = column_sum(contract_cols(grad_both, gate_up))
    ffn_grads = jnp.concatenate(
        [contract_rows(all_feed, grad_both).astype(BF), contract_rows(all_grad, activ).astype(BF)], axis=1
    )
    ffn_sums = lax.psum_scatter(ffn_grads, PLANE, scatter_dimension=0, tiled=True)
    ffn_sums = lax.all_to_all(ffn_sums.reshape(4, shard, 3 * PAD), ("zl", "c"), 0, 0, tiled=True).astype(F32)
    grad_gate_weight = whole_units(ffn_sums[:, :, :PAD])
    grad_up_weight = whole_units(ffn_sums[:, :, PAD : 2 * PAD])
    grad_down = whole_units(ffn_sums[:, :, 2 * PAD :]).T

    hidden_add, feed_terms = norm_back(feed_back, hidden, inv_h, feed_scale)
    grad_hidden = upstream + hidden_add
    grad_branch, post_terms = norm_back(grad_hidden, branch, inv_b, post_gain)
    grad_branch = whole_rows(grad_branch.astype(BF))
    add_all = whole_rows(hidden_add.astype(BF)).astype(F32)
    grad_hidden_all = cotangent.astype(F32) + add_all
    half_gains = jnp.stack([jnp.sum(terms, axis=0) for terms in (post_terms, feed_terms, final_terms)])
    half_gains = half_gains + other_member(half_gains)

    grad_output_t = contract_rows(grad_branch, mixed)
    grad_mixed = product(grad_branch, output_t).astype(BF)
    gm = jnp.stack([grad_mixed[:, :HD], grad_mixed[:, HD:]])
    grad_probs = jnp.einsum("hqd,kd->hqk", gm, values, preferred_element_type=F32)
    center = jnp.sum(probs_f * grad_probs, axis=-1, keepdims=True)
    grad_scores = (probs_f * (grad_probs - center)).astype(BF)
    grad_krot = jnp.einsum("hqk,hqd->kd", grad_scores, q_rot, preferred_element_type=F32) * SCALE
    grad_values = jnp.einsum("hqk,hqd->kd", probs, gm, preferred_element_type=F32)
    kv_part = jnp.concatenate([grad_krot, grad_values], axis=1).astype(BF)
    kv = kv_part.astype(F32) + other_member(kv_part).astype(F32)

    grad_qrot = jnp.einsum("hqk,kd->hqd", grad_scores, k_rot, preferred_element_type=F32) * SCALE
    grad_queries, query_terms = norm_back(rotate(grad_qrot, cosine, -sine), queries, inv_q, query_scale)
    query_gain_part = jnp.sum(query_terms, axis=(0, 1))
    query_gain_sum = query_gain_part + other_member(query_gain_part)
    grad_queries = grad_queries.astype(BF)
    grad_q = jnp.concatenate([grad_queries[0], grad_queries[1]], axis=1)
    normed_part = contract_cols(grad_q, first_half[:, : 2 * HD]).astype(BF)
    normed_q = normed_part.astype(F32) + other_member(normed_part).astype(F32)

    grad_keys, key_terms = norm_back(rotate(kv[:, :HD], cosine, -sine), keys, inv_k, key_scale)
    key_gain_sum = jnp.sum(key_terms, axis=0)
    grad_keys = grad_keys.astype(BF)
    grad_values_low = kv[:, HD:].astype(BF)
    grad_normed = (
        normed_q
        + contract_cols(grad_keys, first_half[:, 2 * HD :])
        + contract_cols(grad_values_low, second_half[:, :HD])
    )
    input_add, input_terms = norm_back(grad_normed, rows, inv_in, norm_gain)
    input_grad = grad_hidden_all + input_add
    input_gain_sum = jnp.sum(input_terms, axis=0)

    grad_qk = contract_rows(normed, jnp.concatenate([grad_q, grad_keys], axis=1)).astype(BF)
    grad_v = contract_rows(normed, grad_values_low).astype(BF)
    head_sums = jnp.pad(
        jnp.concatenate([query_gain_sum.reshape(64, 4), key_gain_sum.reshape(64, 4)], axis=1),
        ((0, 0), (0, shard - 8)),
    ).reshape(1, D)
    gain_sums = jnp.concatenate([input_gain_sum[None], half_gains, head_sums], axis=0).T
    gain_sums = jnp.pad(gain_sums.astype(BF), ((0, 0), (0, 123)))
    side0 = jnp.concatenate([grad_qk, gain_sums], axis=1)
    side1 = jnp.concatenate([grad_v, grad_output_t.astype(BF), jnp.zeros((D, 128), BF)], axis=1)
    keep = jnp.where(core == 0, side0, side1)
    give = jnp.where(core == 0, side1, side0)
    att_sums = (keep.astype(F32) + other_core(give).astype(F32)).astype(BF)
    att_sums = lax.all_to_all(att_sums.reshape(16, 4 * shard, PAD), PLANE, 0, 0, tiled=True)
    att_sums = jnp.sum(att_sums.astype(F32), axis=0).astype(BF)
    att_sums = lax.all_to_all(att_sums.reshape(4, shard, PAD), ("zl", "c"), 0, 0, tiled=True).astype(F32)
    out0 = att_sums[0] + att_sums[2]
    out1 = att_sums[1] + att_sums[3]
    return (
        layer_out,
        input_grad,
        out0[:, 768],
        out0[:, :512],
        out0[:, 512:768],
        out1[:, :256],
        out0[:4, 772],
        out0[4:8, 772],
        out1[:, 256:768].T,
        out0[:, 769],
        out0[:, 770],
        grad_gate_weight,
        grad_up_weight,
        grad_down,
        out0[:, 771],
    )


def solution(mesh):
    fine = Mesh(mesh.devices.reshape(4, 4, 2, 2, 2), ("y", "x", "zl", "c", "t"))
    dp = ("y", "x", "zl", "c")
    in_specs = (
        P(dp, None),
        P(dp, None),
        P(dp),
        P(dp, "t"),
        P(dp, None),
        P(dp, None),
        P(dp),
        P(dp),
        P("t", dp),
        P(dp),
        P(dp),
        P(dp, "t"),
        P(dp, "t"),
        P("t", dp),
        P(dp),
    )
    out_specs = (
        P(dp, None),
        P(dp, None),
        P(dp),
        P(dp, "t"),
        P(dp, None),
        P(dp, None),
        P(dp),
        P(dp),
        P("t", dp),
        P(dp),
        P(dp),
        P(dp, "t"),
        P(dp, "t"),
        P("t", dp),
        P(dp),
    )
    return jax.shard_map(
        on_device, mesh=fine, in_specs=in_specs, out_specs=out_specs, check_vma=False
    )
```

```python
import jax
import jax.numpy as jnp
import numpy as np
from jax import lax
from jax.experimental import pallas as pl
from jax.experimental.pallas import tpu as pltpu
from jax.sharding import Mesh, PartitionSpec as P

D = 1152
HD = 256
SEQ = 256
HALF = SEQ // 2
UNITS = 864
PAD = 896
EPS = 1e-06
THETA = 1000000.0
SCALE = HD ** (-0.5)
BF = jnp.bfloat16
F32 = jnp.float32
PLANE = ("y", "x")


def swap(field, axes, mask, size):
    return lax.ppermute(field, axes, [(i, i ^ mask) for i in range(size)])


def across(field, mask):
    return swap(field, ("zl", "t"), mask, 4)


def other_core(field):
    return swap(field, "c", 1, 2)


def other_member(field):
    return swap(field, "t", 1, 2)


def column_gather(block):
    same = jnp.concatenate([block] + [across(block, m) for m in (1, 2, 3)], axis=0)
    return jnp.concatenate([same, other_core(same)], axis=0)


def column_sum(parts):
    half = parts.shape[0] // 2
    low = parts.astype(BF)
    mine = (low[:half].astype(F32) + other_core(low[half:]).astype(F32)).astype(BF)
    rows = half // 4
    total = mine[:rows].astype(F32)
    for m in (1, 2, 3):
        total = total + across(mine[m * rows : (m + 1) * rows], m).astype(F32)
    return total


def product(left, right):
    return jnp.dot(left, right, preferred_element_type=F32)


def contract_rows(left, right):
    return lax.dot_general(left, right, (((0,), (0,)), ((), ())), preferred_element_type=F32)


def contract_cols(left, right):
    return lax.dot_general(left, right, (((1,), (1,)), ((), ())), preferred_element_type=F32)


def inverse_rms(field):
    return lax.rsqrt(jnp.mean(field * field, axis=-1, keepdims=True) + EPS)


def norm_back(grad, field, inv, gain):
    scaled = grad * gain
    back = inv * scaled - field * (inv * inv * inv) * jnp.mean(field * scaled, axis=-1, keepdims=True)
    return back, grad * field * inv


def tables():
    half = HD // 2
    freq = np.float32(THETA) ** (-np.arange(half, dtype=np.float32) / np.float32(half))
    angle = np.arange(SEQ, dtype=np.float32)[:, None] * freq[None, :].astype(np.float32)
    return jnp.asarray(np.cos(angle).astype(np.float32)), jnp.asarray(np.sin(angle).astype(np.float32))


def rotate(field, cosine, sine):
    half = HD // 2
    first, second = field[..., :half], field[..., half:]
    return jnp.concatenate([first * cosine - second * sine, second * cosine + first * sine], axis=-1)


def head_places():
    place = np.full((2, D), -1, np.int32)
    for row in range(D):
        group, at = divmod(row, 18)
        if at < 8:
            place[at // 4, row] = 4 * group + at % 4
    return jnp.asarray(np.concatenate([place, np.zeros((6, D), np.int32)]))


def one_hot(place_row):
    rows = lax.broadcasted_iota(jnp.int32, (HD, D), 0)
    return jnp.where(rows == place_row, 1.0, 0.0).astype(BF)


def corner():
    rows = lax.broadcasted_iota(jnp.int32, (8, 128), 0)
    return jnp.where(rows == lax.broadcasted_iota(jnp.int32, (8, 128), 1), 1.0, 0.0).astype(BF)


def attend_kernel(
    core, tokens, own, theirs, places, cosine, sine,
    gains, scales, normed_out, qk_out, values_out, rot_out, probs_out, mixed_out, branch_out,
):
    all_gains = contract_cols(corner(), own[:, 768:])
    gains[...] = all_gains
    head_row = all_gains[4:5].astype(BF)
    query_scale = contract_cols(head_row, one_hot(places[0:1]))
    key_scale = contract_cols(head_row, one_hot(places[1:2]))
    scales[...] = jnp.concatenate([query_scale, key_scale, jnp.zeros((6, HD), F32)], axis=0)
    rows = tokens[...].astype(F32)
    normed = (rows * inverse_rms(rows) * all_gains[0:1]).astype(BF)
    normed_out[...] = normed

    def run(first, second):
        cos, sin = cosine[...], sine[...]
        qk = product(normed, first[:, :768])
        qk_out[...] = qk
        values = product(normed, second[:, :HD]).astype(BF)
        values_out[...] = values

        def prepare(field, scale):
            return rotate(field * inverse_rms(field) * scale, cos, sin).astype(BF)

        k_rot = prepare(qk[:, 2 * HD :], key_scale)
        rot_out[:, 2 * HD :] = k_rot
        causal = lax.broadcasted_iota(jnp.int32, (SEQ, SEQ), 1) <= lax.broadcasted_iota(
            jnp.int32, (SEQ, SEQ), 0
        )
        for head in range(2):
            at = slice(head * HD, (head + 1) * HD)
            q_rot = prepare(qk[:, at], query_scale)
            rot_out[:, at] = q_rot
            scores = jnp.where(causal, contract_cols(q_rot, k_rot) * SCALE, -1e30)
            expo = jnp.exp(scores - jnp.max(scores, axis=-1, keepdims=True))
            probs = expo / jnp.sum(expo, axis=-1, keepdims=True)
            probs_out[head] = probs
            mixed_out[:, at] = product(probs.astype(BF), values).astype(BF)
        branch_out[...] = contract_cols(mixed_out[...], second[:, HD:768])

    @pl.when(core[0] == 0)
    def _():
        run(own, theirs)

    @pl.when(core[0] != 0)
    def _():
        run(theirs, own)


def attend_back_kernel(
    core, grad, own, theirs, cosine, sine, scales, qk, values, rot, probs,
    kv_out, grad_q_out, normed_out, query_gain_out,
):
    def run(first, second):
        cos, sin = cosine[...], sine[...]
        query_scale = scales[0:1]
        grad_mixed = product(grad[...], second[:, HD:768]).astype(BF)
        k_rot = rot[:, 2 * HD :]
        low_values = values[...]
        grad_k = jnp.zeros((SEQ, HD), F32)
        grad_v = jnp.zeros((SEQ, HD), F32)
        gain = jnp.zeros((1, HD), F32)
        for head in range(2):
            at = slice(head * HD, (head + 1) * HD)
            weights = probs[head]
            back = grad_mixed[:, at]
            grad_probs = contract_cols(back, low_values)
            center = jnp.sum(weights * grad_probs, axis=-1, keepdims=True)
            grad_scores = (weights * (grad_probs - center)).astype(BF)
            grad_k = grad_k + contract_rows(grad_scores, rot[:, at])
            grad_v = grad_v + contract_rows(weights.astype(BF), back)
            grad_rot = product(grad_scores, k_rot) * SCALE
            field = qk[:, at]
            grad_field, terms = norm_back(
                rotate(grad_rot, cos, -sin), field, inverse_rms(field), query_scale
            )
            gain = gain + jnp.sum(terms, axis=0, keepdims=True)
            grad_q_out[:, at] = grad_field.astype(BF)
        kv_out[:, :HD] = (grad_k * SCALE).astype(BF)
        kv_out[:, HD:] = grad_v.astype(BF)
        query_gain_out[...] = jnp.broadcast_to(gain, (8, HD))
        normed_out[...] = contract_cols(grad_q_out[...], first[:, : 2 * HD]).astype(BF)

    @pl.when(core[0] == 0)
    def _():
        run(own, theirs)

    @pl.when(core[0] != 0)
    def _():
        run(theirs, own)


def finish_kernel(
    core, tokens, cotangent, hidden_add, own, theirs, places, cosine, sine, gains, scales, normed, qk,
    kv_own, kv_their, part_own, part_their, grad_q, query_gain, half_gains, grad_branch, mixed,
    input_grad, keep, give,
):
    kv = kv_own[...].astype(F32) + kv_their[...].astype(F32)
    keys = qk[:, 2 * HD :]
    grad_keys, key_terms = norm_back(
        rotate(kv[:, :HD], cosine[...], -sine[...]), keys, inverse_rms(keys), scales[1:2]
    )
    key_gain = jnp.sum(key_terms, axis=0, keepdims=True)
    grad_keys = grad_keys.astype(BF)
    grad_values = kv[:, HD:].astype(BF)

    def run(first, second, side0, side1):
        grad_normed = (
            part_own[...].astype(F32)
            + part_their[...].astype(F32)
            + contract_cols(grad_keys, first[:, 2 * HD : 768])
            + contract_cols(grad_values, second[:, :HD])
        )
        rows = tokens[...].astype(F32)
        add, terms = norm_back(grad_normed, rows, inverse_rms(rows), gains[0:1])
        input_grad[...] = cotangent[...].astype(F32) + hidden_add[...].astype(F32) + add
        input_gain = jnp.sum(terms, axis=0, keepdims=True)
        low = jnp.concatenate([query_gain[0:1], key_gain], axis=1).astype(BF)
        head_row = product(low[:, :HD], one_hot(places[0:1])) + product(low[:, HD:], one_hot(places[1:2]))
        sums = jnp.concatenate(
            [input_gain, half_gains[0:3], head_row, jnp.zeros((3, D), F32)], axis=0
        ).astype(BF)
        side0[:, 768:] = contract_rows(sums, corner()).astype(BF)
        side1[:, 768:] = jnp.zeros((D, 128), BF)
        turned = normed[...]
        side0[:, : 2 * HD] = contract_rows(turned, grad_q[...]).astype(BF)
        side0[:, 2 * HD : 768] = contract_rows(turned, grad_keys).astype(BF)
        side1[:, :HD] = contract_rows(turned, grad_values).astype(BF)
        side1[:, HD:768] = contract_rows(grad_branch[...], mixed[...]).astype(BF)

    @pl.when(core[0] == 0)
    def _():
        run(own, theirs, keep, give)

    @pl.when(core[0] != 0)
    def _():
        run(theirs, own, give, keep)


def local(kernel, outs, count, flops):
    shapes = [jax.ShapeDtypeStruct(shape, dtype) for shape, dtype in outs]
    return pl.pallas_call(
        kernel,
        out_shape=shapes,
        in_specs=[pl.BlockSpec(memory_space=pltpu.SMEM)]
        + [pl.BlockSpec(memory_space=pltpu.VMEM)] * count,
        out_specs=[pl.BlockSpec(memory_space=pltpu.VMEM)] * len(outs),
        compiler_params=pltpu.CompilerParams(vmem_limit_bytes=48 * 2**20),
        cost_estimate=pl.CostEstimate(flops=flops, bytes_accessed=8 * 2**20, transcendentals=200000),
    )


def quarters(weight):
    cut = weight.reshape(weight.shape[0], 4, UNITS).transpose(1, 0, 2)
    return jnp.pad(cut, ((0, 0), (0, 0), (0, PAD - UNITS)))


def whole_units(block):
    return block[:, :, :UNITS].transpose(1, 0, 2).reshape(block.shape[1], 4 * UNITS)


def on_device(
    tokens,
    cotangent,
    input_gain,
    query_weight,
    key_weight,
    value_weight,
    query_gain,
    key_gain,
    output_weight,
    attention_gain,
    feed_gain,
    gate_weight,
    up_weight,
    down_weight,
    output_gain,
):
    core = lax.axis_index("c")
    member = lax.axis_index("t")
    shard = input_gain.shape[0]
    heads_gain = jnp.concatenate([query_gain, key_gain, jnp.zeros((shard - 8,), BF)])
    gains = jnp.stack([input_gain, attention_gain, feed_gain, output_gain, heads_gain], axis=1)
    gains = jnp.pad(gains, ((0, 0), (0, 123)))
    half0 = jnp.concatenate([query_weight, key_weight, gains], axis=1)
    half1 = jnp.concatenate([value_weight, output_weight.T, gains], axis=1)
    pack = jnp.concatenate(
        [
            jnp.stack([half0, half1, half0, half1]),
            quarters(gate_weight),
            quarters(up_weight),
            quarters(down_weight.T),
        ],
        axis=2,
    )
    got = lax.all_to_all(pack, ("zl", "c"), 0, 0, tiled=True).reshape(4 * shard, -1)
    att_shard = got[:, :PAD]
    att_half = lax.all_to_all(
        jnp.broadcast_to(att_shard[None], (16, *att_shard.shape)), PLANE, 0, 0, tiled=True
    ).reshape(D, PAD)
    feed_weights = lax.all_gather(got[:, PAD:], PLANE, axis=0, tiled=True)

    flag = jnp.reshape(core, (1,)).astype(jnp.int32)
    their_half = other_core(att_half[:, :768])
    cosine, sine = tables()
    places = head_places()
    gains, scales, normed, qk, values, rot, probs_f, mixed, branch_part = local(
        attend_kernel,
        [
            ((8, D), F32), ((8, HD), F32), ((SEQ, D), BF), ((SEQ, 768), F32), ((SEQ, HD), BF),
            ((SEQ, 768), BF), ((2, SEQ, SEQ), F32), ((SEQ, 2 * HD), BF), ((SEQ, D), F32),
        ],
        6,
        1100000000,
    )(flag, tokens, att_half, their_half, places, cosine, sine)
    post_gain, feed_scale, final_gain = (gains[i : i + 1] for i in (1, 2, 3))

    def my_half(field):
        return lax.dynamic_slice_in_dim(field, member * HALF, HALF, 0)

    def their_rows(field):
        return lax.dynamic_slice_in_dim(field, (1 - member) * HALF, HALF, 0)

    def whole_rows(field):
        theirs = other_member(field)
        top = jnp.where(member == 0, field, theirs)
        bottom = jnp.where(member == 0, theirs, field)
        return jnp.concatenate([top, bottom], axis=0)

    branch = my_half(branch_part) + other_member(their_rows(branch_part).astype(BF)).astype(F32)
    my_rows = my_half(tokens).astype(F32)
    inv_b = inverse_rms(branch)
    hidden = my_rows + branch * inv_b * post_gain
    inv_h = inverse_rms(hidden)
    feed = (hidden * inv_h * feed_scale).astype(BF)

    all_feed = column_gather(feed)
    gate_up = feed_weights[:, : 2 * PAD]
    down_t = feed_weights[:, 2 * PAD :]
    both = product(all_feed, gate_up)
    gate, upper = both[:, :PAD], both[:, PAD:]
    k0 = np.float32(np.sqrt(2.0 / np.pi))
    square = gate * gate
    tanh = jnp.tanh(k0 * gate * (1.0 + 0.044715 * square))
    gelu = 0.5 * gate * (1.0 + tanh)
    slope = 0.5 * (1.0 + tanh) + 0.5 * gate * (1.0 - tanh * tanh) * (k0 * (1.0 + 3 * 0.044715 * square))
    activ = (gelu * upper).astype(BF)
    second = column_sum(contract_cols(activ, down_t))
    inv_s = inverse_rms(second)
    layer_half = (hidden + second * inv_s * final_gain).astype(BF)
    layer_out = whole_rows(layer_half)

    upstream = my_half(cotangent).astype(F32)
    grad_second, final_terms = norm_back(upstream, second, inv_s, final_gain)
    all_grad = column_gather(grad_second.astype(BF))
    grad_activ = product(all_grad, down_t)
    grad_gate = (grad_activ * upper * slope).astype(BF)
    grad_upper = (grad_activ * gelu).astype(BF)
    grad_both = jnp.concatenate([grad_gate, grad_upper], axis=1)
    feed_back = column_sum(contract_cols(grad_both, gate_up))
    ffn_grads = jnp.concatenate(
        [contract_rows(all_feed, grad_both).astype(BF), contract_rows(all_grad, activ).astype(BF)], axis=1
    )
    ffn_sums = lax.psum_scatter(ffn_grads, PLANE, scatter_dimension=0, tiled=True)
    hidden_add, feed_terms = norm_back(feed_back, hidden, inv_h, feed_scale)
    grad_hidden = upstream + hidden_add
    grad_branch, post_terms = norm_back(grad_hidden, branch, inv_b, post_gain)
    grad_branch = whole_rows(grad_branch.astype(BF))
    add_all = whole_rows(hidden_add.astype(BF))
    half_gains = jnp.stack([jnp.sum(terms, axis=0) for terms in (post_terms, feed_terms, final_terms)])
    half_gains = jnp.pad(half_gains, ((0, 5), (0, 0)))
    half_gains = half_gains + other_member(half_gains)

    kv_part, grad_q, normed_part, query_gain_part = local(
        attend_back_kernel,
        [((SEQ, 2 * HD), BF), ((SEQ, 2 * HD), BF), ((SEQ, D), BF), ((8, HD), F32)],
        10,
        1100000000,
    )(flag, grad_branch, att_half, their_half, cosine, sine, scales, qk, values, rot, probs_f)
    kv_their = other_member(kv_part)
    normed_their = other_member(normed_part)
    query_gain_sum = query_gain_part + other_member(query_gain_part)
    input_grad, keep, give = local(
        finish_kernel,
        [((SEQ, D), F32), ((D, PAD), BF), ((D, PAD), BF)],
        21,
        1300000000,
    )(
        flag, tokens, cotangent, add_all, att_half, their_half, places, cosine, sine, gains, scales, normed, qk,
        kv_part, kv_their, normed_part, normed_their, grad_q, query_gain_sum, half_gains, grad_branch, mixed,
    )
    att_sums = (keep.astype(F32) + other_core(give).astype(F32)).astype(BF)
    att_sums = lax.all_to_all(att_sums.reshape(16, 4 * shard, PAD), PLANE, 0, 0, tiled=True)
    att_sums = jnp.sum(att_sums.astype(F32), axis=0).astype(BF)
    att_sums = lax.all_to_all(att_sums.reshape(4, shard, PAD), ("zl", "c"), 0, 0, tiled=True).astype(F32)
    out0 = att_sums[0] + att_sums[2]
    out1 = att_sums[1] + att_sums[3]

    blocks = ffn_sums.reshape(4, shard, 3 * PAD)
    place = 2 * lax.axis_index("zl") + core
    pieces = []
    for mask in range(4):
        block = lax.dynamic_index_in_dim(blocks, place ^ mask, 0, keepdims=False)
        pieces.append(block if mask == 0 else swap(block, ("zl", "c"), mask, 4))
    arrived = jnp.stack(pieces)
    ffn_sums = jnp.stack(
        [lax.dynamic_index_in_dim(arrived, place ^ k, 0, keepdims=False) for k in range(4)]
    ).astype(F32)
    grad_gate_weight = whole_units(ffn_sums[:, :, :PAD])
    grad_up_weight = whole_units(ffn_sums[:, :, PAD : 2 * PAD])
    grad_down = whole_units(ffn_sums[:, :, 2 * PAD :]).T
    return (
        layer_out,
        input_grad,
        out0[:, 768],
        out0[:, :512],
        out0[:, 512:768],
        out1[:, :256],
        out0[:4, 772],
        out0[4:8, 772],
        out1[:, 256:768].T,
        out0[:, 769],
        out0[:, 770],
        grad_gate_weight,
        grad_up_weight,
        grad_down,
        out0[:, 771],
    )


def solution(mesh):
    fine = Mesh(mesh.devices.reshape(4, 4, 2, 2, 2), ("y", "x", "zl", "c", "t"))
    dp = ("y", "x", "zl", "c")
    in_specs = (
        P(dp, None),
        P(dp, None),
        P(dp),
        P(dp, "t"),
        P(dp, None),
        P(dp, None),
        P(dp),
        P(dp),
        P("t", dp),
        P(dp),
        P(dp),
        P(dp, "t"),
        P(dp, "t"),
        P("t", dp),
        P(dp),
    )
    out_specs = (
        P(dp, None),
        P(dp, None),
        P(dp),
        P(dp, "t"),
        P(dp, None),
        P(dp, None),
        P(dp),
        P(dp),
        P("t", dp),
        P(dp),
        P(dp),
        P(dp, "t"),
        P(dp, "t"),
        P("t", dp),
        P(dp),
    )
    return jax.shard_map(
        on_device, mesh=fine, in_specs=in_specs, out_specs=out_specs, check_vma=False
    )
```

```python
import jax
import jax.numpy as jnp
import numpy as np
from jax import lax
from jax.experimental import pallas as pl
from jax.experimental.pallas import tpu as pltpu
from jax.sharding import Mesh, PartitionSpec as P

D = 1152
HD = 256
SEQ = 256
HALF = SEQ // 2
UNITS = 864
VALUES = 768
MIXED = 1024
PAD = 896
EPS = 1e-06
THETA = 1000000.0
SCALE = HD ** (-0.5)
BF = jnp.bfloat16
F32 = jnp.float32
PLANE = ("y", "x")


def swap(field, axes, mask, size):
    return lax.ppermute(field, axes, [(i, i ^ mask) for i in range(size)])


def across(field, mask):
    return swap(field, ("zl", "t"), mask, 4)


def other_core(field):
    return swap(field, "c", 1, 2)


def other_member(field):
    return swap(field, "t", 1, 2)


def column_gather(block):
    same = jnp.concatenate([block] + [across(block, m) for m in (1, 2, 3)], axis=0)
    return jnp.concatenate([same, other_core(same)], axis=0)


def column_sum(parts):
    half = parts.shape[0] // 2
    low = parts.astype(BF)
    mine = (low[:half].astype(F32) + other_core(low[half:]).astype(F32)).astype(BF)
    rows = half // 4
    total = mine[:rows].astype(F32)
    for m in (1, 2, 3):
        total = total + across(mine[m * rows : (m + 1) * rows], m).astype(F32)
    return total


def product(left, right):
    return jnp.dot(left, right, preferred_element_type=F32)


def contract_rows(left, right):
    return lax.dot_general(left, right, (((0,), (0,)), ((), ())), preferred_element_type=F32)


def contract_cols(left, right):
    return lax.dot_general(left, right, (((1,), (1,)), ((), ())), preferred_element_type=F32)


def inverse_rms(field):
    return lax.rsqrt(jnp.mean(field * field, axis=-1, keepdims=True) + EPS)


def norm_back(grad, field, inv, gain):
    scaled = grad * gain
    back = inv * scaled - field * (inv * inv * inv) * jnp.mean(field * scaled, axis=-1, keepdims=True)
    return back, grad * field * inv


def tables():
    half = HD // 2
    freq = np.float32(THETA) ** (-np.arange(half, dtype=np.float32) / np.float32(half))
    angle = np.arange(SEQ, dtype=np.float32)[:, None] * freq[None, :].astype(np.float32)
    return jnp.asarray(np.cos(angle).astype(np.float32)), jnp.asarray(np.sin(angle).astype(np.float32))


def rotate(field, cosine, sine):
    half = HD // 2
    first, second = field[..., :half], field[..., half:]
    return jnp.concatenate([first * cosine - second * sine, second * cosine + first * sine], axis=-1)


def head_places():
    place = np.full((2, D), -1, np.int32)
    for row in range(D):
        group, at = divmod(row, 18)
        if at < 8:
            place[at // 4, row] = 4 * group + at % 4
    return jnp.asarray(np.concatenate([place, np.zeros((6, D), np.int32)]))


def one_hot(place_row):
    rows = lax.broadcasted_iota(jnp.int32, (HD, D), 0)
    return jnp.where(rows == place_row, 1.0, 0.0).astype(BF)


def corner():
    rows = lax.broadcasted_iota(jnp.int32, (8, 128), 0)
    return jnp.where(rows == lax.broadcasted_iota(jnp.int32, (8, 128), 1), 1.0, 0.0).astype(BF)


def attend_kernel(
    place, tokens, own, theirs, places, cosine, sine,
    gains, kept, kept_f, probs_out, branch_mine, branch_give,
):
    all_gains = contract_cols(corner(), own[:, 768:])
    head_row = all_gains[4:5].astype(BF)
    query_scale = contract_cols(head_row, one_hot(places[0:1]))
    key_scale = contract_cols(head_row, one_hot(places[1:2]))
    gains[:, :D] = all_gains
    gains[:, D:] = jnp.concatenate([query_scale, key_scale, jnp.zeros((6, HD), F32)], axis=0)
    rows = tokens[...].astype(F32)
    normed = (rows * inverse_rms(rows) * all_gains[0:1]).astype(BF)
    kept[:, MIXED + 2 * HD :] = normed

    def run(first, second):
        cos, sin = cosine[...], sine[...]
        qk = product(normed, first[:, :768])
        kept_f[...] = qk
        values = product(normed, second[:, :HD]).astype(BF)
        kept[:, VALUES:MIXED] = values

        def prepare(field, scale):
            return rotate(field * inverse_rms(field) * scale, cos, sin).astype(BF)

        k_rot = prepare(qk[:, 2 * HD :], key_scale)
        kept[:, 2 * HD : VALUES] = k_rot
        causal = lax.broadcasted_iota(jnp.int32, (SEQ, SEQ), 1) <= lax.broadcasted_iota(
            jnp.int32, (SEQ, SEQ), 0
        )
        for head in range(2):
            at = slice(head * HD, (head + 1) * HD)
            q_rot = prepare(qk[:, at], query_scale)
            kept[:, at] = q_rot
            scores = jnp.where(causal, contract_cols(q_rot, k_rot) * SCALE, -1e30)
            expo = jnp.exp(scores - jnp.max(scores, axis=-1, keepdims=True))
            probs = expo / jnp.sum(expo, axis=-1, keepdims=True)
            probs_out[head] = probs
            kept[:, MIXED + head * HD : MIXED + (head + 1) * HD] = product(probs.astype(BF), values).astype(BF)
        mine = pl.multiple_of(place[1] * HALF, HALF)
        give = pl.multiple_of((1 - place[1]) * HALF, HALF)
        mixed = MIXED + 2 * HD
        branch_mine[...] = contract_cols(kept[pl.ds(mine, HALF), MIXED:mixed], second[:, HD:768])
        branch_give[...] = contract_cols(kept[pl.ds(give, HALF), MIXED:mixed], second[:, HD:768]).astype(BF)

    @pl.when(place[0] == 0)
    def _():
        run(own, theirs)

    @pl.when(place[0] != 0)
    def _():
        run(theirs, own)


def attend_back_kernel(
    place, grad, own, theirs, cosine, sine, gains, kept, kept_f, probs,
    kv_out, grad_q_out, normed_mine, normed_give, query_gain_out,
):
    def run(first, second):
        cos, sin = cosine[...], sine[...]
        query_scale = gains[0:1, D:]
        grad_mixed = product(grad[...], second[:, HD:768]).astype(BF)
        k_rot = kept[:, 2 * HD : VALUES]
        low_values = kept[:, VALUES:MIXED]
        grad_k = jnp.zeros((SEQ, HD), F32)
        grad_v = jnp.zeros((SEQ, HD), F32)
        gain = jnp.zeros((1, HD), F32)
        for head in range(2):
            at = slice(head * HD, (head + 1) * HD)
            weights = probs[head]
            back = grad_mixed[:, at]
            grad_probs = contract_cols(back, low_values)
            center = jnp.sum(weights * grad_probs, axis=-1, keepdims=True)
            grad_scores = (weights * (grad_probs - center)).astype(BF)
            grad_k = grad_k + contract_rows(grad_scores, kept[:, at])
            grad_v = grad_v + contract_rows(weights.astype(BF), back)
            grad_rot = product(grad_scores, k_rot) * SCALE
            field = kept_f[:, at]
            grad_field, terms = norm_back(
                rotate(grad_rot, cos, -sin), field, inverse_rms(field), query_scale
            )
            gain = gain + jnp.sum(terms, axis=0, keepdims=True)
            grad_q_out[:, at] = grad_field.astype(BF)
        kv_out[:, :HD] = (grad_k * SCALE).astype(BF)
        kv_out[:, HD:] = grad_v.astype(BF)
        query_gain_out[...] = jnp.broadcast_to(gain, (8, HD))
        mine = pl.multiple_of(place[1] * HALF, HALF)
        give = pl.multiple_of((1 - place[1]) * HALF, HALF)
        normed_mine[...] = contract_cols(grad_q_out[pl.ds(mine, HALF), :], first[:, : 2 * HD])
        normed_give[...] = contract_cols(grad_q_out[pl.ds(give, HALF), :], first[:, : 2 * HD]).astype(BF)

    @pl.when(place[0] == 0)
    def _():
        run(own, theirs)

    @pl.when(place[0] != 0)
    def _():
        run(theirs, own)


def input_kernel(
    place, tokens, grad_hidden, own, theirs, places, cosine, sine, gains, kept_f,
    kv_own, kv_their, part_mine, part_their, query_gain, half_gains,
    input_half, grad_kv, gain_rows,
):
    kv = kv_own[...].astype(F32) + kv_their[...].astype(F32)
    keys = kept_f[:, 2 * HD :]
    grad_keys, key_terms = norm_back(
        rotate(kv[:, :HD], cosine[...], -sine[...]), keys, inverse_rms(keys), gains[1:2, D:]
    )
    key_gain = 0.5 * jnp.sum(key_terms, axis=0, keepdims=True)
    grad_kv[:, :HD] = grad_keys.astype(BF)
    grad_kv[:, HD:] = kv[:, HD:].astype(BF)
    low = jnp.concatenate([query_gain[0:1], key_gain], axis=1)
    high = low.astype(BF)
    rest = (low - high.astype(F32)).astype(BF)

    def spread(part):
        return product(part[:, :HD], one_hot(places[0:1])) + product(part[:, HD:], one_hot(places[1:2]))

    head_row = spread(high) + spread(rest)
    mine = pl.multiple_of(place[1] * HALF, HALF)

    def run(first, second):
        grad_normed = (
            part_mine[...]
            + part_their[...].astype(F32)
            + contract_cols(grad_kv[pl.ds(mine, HALF), :HD], first[:, 2 * HD : 768])
            + contract_cols(grad_kv[pl.ds(mine, HALF), HD:], second[:, :HD])
        )
        rows = tokens[pl.ds(mine, HALF), :].astype(F32)
        add, terms = norm_back(grad_normed, rows, inverse_rms(rows), gains[0:1, :D])
        input_half[...] = grad_hidden[...] + add
        input_gain = jnp.sum(terms, axis=0, keepdims=True)
        gain_rows[...] = jnp.concatenate(
            [input_gain, half_gains[0:3], head_row, jnp.zeros((3, D), F32)], axis=0
        )

    @pl.when(place[0] == 0)
    def _():
        run(own, theirs)

    @pl.when(place[0] != 0)
    def _():
        run(theirs, own)


def weights_kernel(place, kept, grad_q, grad_kv, grad_branch, keep, give):
    normed = kept[:, MIXED + 2 * HD :]

    def run(side0, side1):
        side0[:, : 2 * HD] = contract_rows(normed, grad_q[...]).astype(BF)
        side0[:, 2 * HD :] = contract_rows(normed, grad_kv[:, :HD]).astype(BF)
        side1[:, :HD] = contract_rows(normed, grad_kv[:, HD:]).astype(BF)
        side1[:, HD:] = contract_rows(grad_branch[...], kept[:, MIXED : MIXED + 2 * HD]).astype(BF)

    @pl.when(place[0] == 0)
    def _():
        run(keep, give)

    @pl.when(place[0] != 0)
    def _():
        run(give, keep)


def local(kernel, outs, count, flops):
    shapes = [jax.ShapeDtypeStruct(shape, dtype) for shape, dtype in outs]
    return pl.pallas_call(
        kernel,
        out_shape=shapes,
        in_specs=[pl.BlockSpec(memory_space=pltpu.SMEM)]
        + [pl.BlockSpec(memory_space=pltpu.VMEM)] * count,
        out_specs=[pl.BlockSpec(memory_space=pltpu.VMEM)] * len(outs),
        compiler_params=pltpu.CompilerParams(vmem_limit_bytes=48 * 2**20),
        cost_estimate=pl.CostEstimate(flops=flops, bytes_accessed=8 * 2**20, transcendentals=200000),
    )


def column_cut(blocks, place):
    pieces = []
    for mask in range(4):
        block = lax.dynamic_index_in_dim(blocks, place ^ mask, 0, keepdims=False)
        pieces.append(block if mask == 0 else swap(block, ("zl", "c"), mask, 4))
    arrived = jnp.stack(pieces)
    return jnp.stack([lax.dynamic_index_in_dim(arrived, place ^ k, 0, keepdims=False) for k in range(4)])


def quarters(weight):
    cut = weight.reshape(weight.shape[0], 4, UNITS).transpose(1, 0, 2)
    return jnp.pad(cut, ((0, 0), (0, 0), (0, PAD - UNITS)))


def whole_units(block):
    return block[:, :, :UNITS].transpose(1, 0, 2).reshape(block.shape[1], 4 * UNITS)


def on_device(
    tokens,
    cotangent,
    input_gain,
    query_weight,
    key_weight,
    value_weight,
    query_gain,
    key_gain,
    output_weight,
    attention_gain,
    feed_gain,
    gate_weight,
    up_weight,
    down_weight,
    output_gain,
):
    core = lax.axis_index("c")
    member = lax.axis_index("t")
    shard = input_gain.shape[0]
    heads_gain = jnp.concatenate([query_gain, key_gain, jnp.zeros((shard - 8,), BF)])
    gains = jnp.stack([input_gain, attention_gain, feed_gain, output_gain, heads_gain], axis=1)
    gains = jnp.pad(gains, ((0, 0), (0, 123)))
    half0 = jnp.concatenate([query_weight, key_weight, gains], axis=1)
    half1 = jnp.concatenate([value_weight, output_weight.T, gains], axis=1)
    column = 2 * lax.axis_index("zl") + core
    att_pack = jnp.stack([half0, half1, half0, half1])
    att_shard = lax.all_to_all(att_pack, ("zl", "c"), 0, 0, tiled=True).reshape(4 * shard, PAD)
    ffn_pack = jnp.concatenate(
        [quarters(gate_weight), quarters(up_weight), quarters(down_weight.T)], axis=2
    )
    ffn_shard = column_cut(ffn_pack, column).reshape(4 * shard, 3 * PAD)
    att_half = lax.all_to_all(
        jnp.broadcast_to(att_shard[None], (16, *att_shard.shape)), PLANE, 0, 0, tiled=True
    ).reshape(D, PAD)
    att_half, ffn_shard = lax.optimization_barrier((att_half, ffn_shard))
    feed_weights = lax.all_gather(ffn_shard, PLANE, axis=0, tiled=True)

    flag = jnp.stack([core, member]).astype(jnp.int32)
    their_half = other_core(att_half[:, :768])
    cosine, sine = tables()
    places = head_places()
    gains, kept, kept_f, probs_f, branch_mine, branch_give = local(
        attend_kernel,
        [
            ((8, D + HD), F32), ((SEQ, MIXED + 2 * HD + D), BF), ((SEQ, 768), F32), ((2, SEQ, SEQ), F32),
            ((HALF, D), F32), ((HALF, D), BF),
        ],
        6,
        1100000000,
    )(flag, tokens, att_half, their_half, places, cosine, sine)
    post_gain, feed_scale, final_gain = (gains[i : i + 1, :D] for i in (1, 2, 3))

    def my_half(field):
        return lax.dynamic_slice_in_dim(field, member * HALF, HALF, 0)

    def whole_rows(field):
        theirs = other_member(field)
        top = jnp.where(member == 0, field, theirs)
        bottom = jnp.where(member == 0, theirs, field)
        return jnp.concatenate([top, bottom], axis=0)

    branch = branch_mine + other_member(branch_give).astype(F32)
    my_rows = my_half(tokens).astype(F32)
    inv_b = inverse_rms(branch)
    hidden = my_rows + branch * inv_b * post_gain
    inv_h = inverse_rms(hidden)
    feed = (hidden * inv_h * feed_scale).astype(BF)

    all_feed = column_gather(feed)
    gate_up = feed_weights[:, : 2 * PAD]
    down_t = feed_weights[:, 2 * PAD :]
    both = product(all_feed, gate_up)
    gate, upper = both[:, :PAD], both[:, PAD:]
    k0 = np.float32(np.sqrt(2.0 / np.pi))
    square = gate * gate
    tanh = jnp.tanh(k0 * gate * (1.0 + 0.044715 * square))
    gelu = 0.5 * gate * (1.0 + tanh)
    slope = 0.5 * (1.0 + tanh) + 0.5 * gate * (1.0 - tanh * tanh) * (k0 * (1.0 + 3 * 0.044715 * square))
    activ = (gelu * upper).astype(BF)
    second = column_sum(contract_cols(activ, down_t))
    inv_s = inverse_rms(second)
    layer_half = (hidden + second * inv_s * final_gain).astype(BF)
    layer_out = whole_rows(layer_half)

    upstream = my_half(cotangent).astype(F32)
    grad_second, final_terms = norm_back(upstream, second, inv_s, final_gain)
    all_grad = column_gather(grad_second.astype(BF))
    grad_activ = product(all_grad, down_t)
    grad_gate = (grad_activ * upper * slope).astype(BF)
    grad_upper = (grad_activ * gelu).astype(BF)
    grad_both = jnp.concatenate([grad_gate, grad_upper], axis=1)
    feed_back = column_sum(contract_cols(grad_both, gate_up))
    ffn_grads = jnp.concatenate(
        [contract_rows(all_feed, grad_both).astype(BF), contract_rows(all_grad, activ).astype(BF)], axis=1
    )
    ffn_sums = lax.psum_scatter(ffn_grads, PLANE, scatter_dimension=0, tiled=True)
    hidden_add, feed_terms = norm_back(feed_back, hidden, inv_h, feed_scale)
    grad_hidden = upstream + hidden_add
    grad_branch, post_terms = norm_back(grad_hidden, branch, inv_b, post_gain)
    grad_branch = whole_rows(grad_branch.astype(BF))
    half_gains = jnp.stack([jnp.sum(terms, axis=0) for terms in (post_terms, feed_terms, final_terms)])
    half_gains = jnp.pad(half_gains, ((0, 5), (0, 0)))

    kv_part, grad_q, normed_mine, normed_give, query_gain = local(
        attend_back_kernel,
        [
            ((SEQ, 2 * HD), BF), ((SEQ, 2 * HD), BF), ((HALF, D), F32), ((HALF, D), BF), ((8, HD), F32),
        ],
        9,
        1100000000,
    )(flag, grad_branch, att_half, their_half, cosine, sine, gains, kept, kept_f, probs_f)
    input_half, grad_kv, gain_rows = local(
        input_kernel,
        [((HALF, D), F32), ((SEQ, 2 * HD), BF), ((8, D), F32)],
        15,
        400000000,
    )(
        flag, tokens, grad_hidden, att_half, their_half, places, cosine, sine, gains, kept_f,
        kv_part, other_member(kv_part), normed_mine, other_member(normed_give), query_gain, half_gains,
    )
    keep, give = local(weights_kernel, [((D, 768), BF), ((D, 768), BF)], 4, 900000000)(
        flag, kept, grad_q, grad_kv, grad_branch
    )
    gain_sums = (gain_rows + swap(gain_rows, ("c", "t"), 2, 4)) + (
        swap(gain_rows, ("c", "t"), 1, 4) + swap(gain_rows, ("c", "t"), 3, 4)
    )
    gain_cols = jnp.pad(gain_sums.T.astype(BF), ((0, 0), (0, 120)))
    att_sums = (keep.astype(F32) + other_core(give).astype(F32)).astype(BF)
    att_sums = jnp.concatenate([att_sums, gain_cols], axis=1)
    blocks = ffn_sums.reshape(4, shard, 3 * PAD)
    blocks, att_sums = lax.optimization_barrier((blocks, att_sums))
    ffn_sums = column_cut(blocks, column).astype(F32)
    grad_gate_weight = whole_units(ffn_sums[:, :, :PAD])
    grad_up_weight = whole_units(ffn_sums[:, :, PAD : 2 * PAD])
    grad_down = whole_units(ffn_sums[:, :, 2 * PAD :]).T
    input_grad = whole_rows(input_half)
    att_sums = lax.all_to_all(att_sums.reshape(16, 4 * shard, PAD), PLANE, 0, 0, tiled=True)
    att_sums = jnp.sum(att_sums.astype(F32), axis=0).astype(BF)
    att_sums = lax.all_to_all(att_sums.reshape(4, shard, PAD), ("zl", "c"), 0, 0, tiled=True).astype(F32)
    out0 = att_sums[0] + att_sums[2]
    out1 = att_sums[1] + att_sums[3]

    return (
        layer_out,
        input_grad,
        out0[:, 768],
        out0[:, :512],
        out0[:, 512:768],
        out1[:, :256],
        out0[:4, 772],
        out0[4:8, 772],
        out1[:, 256:768].T,
        out0[:, 769],
        out0[:, 770],
        grad_gate_weight,
        grad_up_weight,
        grad_down,
        out0[:, 771],
    )


def solution(mesh):
    fine = Mesh(mesh.devices.reshape(4, 4, 2, 2, 2), ("y", "x", "zl", "c", "t"))
    dp = ("y", "x", "zl", "c")
    in_specs = (
        P(dp, None),
        P(dp, None),
        P(dp),
        P(dp, "t"),
        P(dp, None),
        P(dp, None),
        P(dp),
        P(dp),
        P("t", dp),
        P(dp),
        P(dp),
        P(dp, "t"),
        P(dp, "t"),
        P("t", dp),
        P(dp),
    )
    out_specs = (
        P(dp, None),
        P(dp, None),
        P(dp),
        P(dp, "t"),
        P(dp, None),
        P(dp, None),
        P(dp),
        P(dp),
        P("t", dp),
        P(dp),
        P(dp),
        P(dp, "t"),
        P(dp, "t"),
        P("t", dp),
        P(dp),
    )
    return jax.shard_map(
        on_device, mesh=fine, in_specs=in_specs, out_specs=out_specs, check_vma=False
    )
```

```python
import jax
import jax.numpy as jnp
import numpy as np
from jax import lax
from jax.experimental import pallas as pl
from jax.experimental.pallas import tpu as pltpu
from jax.sharding import Mesh, PartitionSpec as P

D = 1152
HD = 256
SEQ = 256
HALF = SEQ // 2
UNITS = 864
VALUES = 768
MIXED = 1024
PAD = 896
EPS = 1e-06
THETA = 1000000.0
SCALE = HD ** (-0.5)
BF = jnp.bfloat16
F32 = jnp.float32
PLANE = ("y", "x")


def swap(field, axes, mask, size):
    return lax.ppermute(field, axes, [(i, i ^ mask) for i in range(size)])


def across(field, mask):
    return swap(field, ("zl", "t"), mask, 4)


def other_core(field):
    return swap(field, "c", 1, 2)


def other_member(field):
    return swap(field, "t", 1, 2)


def gathered(block):
    near = (block, other_core(block))
    far = [across(block, m) for m in (1, 2, 3)]
    return near, (*far, other_core(jnp.concatenate(far, axis=0)))


def summed(near, far):
    mine = (far[0] + other_core(far[1]).astype(F32)).astype(BF)
    total = near[0] + other_core(near[1]).astype(F32)
    for m in (1, 2, 3):
        total = total + across(mine[(m - 1) * HALF : m * HALF], m).astype(F32)
    return total


def product(left, right):
    return jnp.dot(left, right, preferred_element_type=F32)


def contract_rows(left, right):
    return lax.dot_general(left, right, (((0,), (0,)), ((), ())), preferred_element_type=F32)


def contract_cols(left, right):
    return lax.dot_general(left, right, (((1,), (1,)), ((), ())), preferred_element_type=F32)


def inverse_rms(field):
    return lax.rsqrt(jnp.mean(field * field, axis=-1, keepdims=True) + EPS)


def norm_back(grad, field, inv, gain):
    scaled = grad * gain
    back = inv * scaled - field * (inv * inv * inv) * jnp.mean(field * scaled, axis=-1, keepdims=True)
    return back, grad * field * inv


def tables():
    half = HD // 2
    freq = np.float32(THETA) ** (-np.arange(half, dtype=np.float32) / np.float32(half))
    angle = np.arange(SEQ, dtype=np.float32)[:, None] * freq[None, :].astype(np.float32)
    return jnp.asarray(np.cos(angle).astype(np.float32)), jnp.asarray(np.sin(angle).astype(np.float32))


def rotate(field, cosine, sine):
    half = HD // 2
    first, second = field[..., :half], field[..., half:]
    return jnp.concatenate([first * cosine - second * sine, second * cosine + first * sine], axis=-1)


def head_places():
    place = np.full((2, D), -1, np.int32)
    for row in range(D):
        group, at = divmod(row, 18)
        if at < 8:
            place[at // 4, row] = 4 * group + at % 4
    return jnp.asarray(np.concatenate([place, np.zeros((6, D), np.int32)]))


def one_hot(place_row):
    rows = lax.broadcasted_iota(jnp.int32, (HD, D), 0)
    return jnp.where(rows == place_row, 1.0, 0.0).astype(BF)


def corner():
    rows = lax.broadcasted_iota(jnp.int32, (8, 128), 0)
    return jnp.where(rows == lax.broadcasted_iota(jnp.int32, (8, 128), 1), 1.0, 0.0).astype(BF)


def attend_kernel(
    place, tokens, own, theirs, places, cosine, sine,
    gains, kept, kept_f, probs_out, branch_mine, branch_give,
):
    all_gains = contract_cols(corner(), own[:, 768:])
    head_row = all_gains[4:5].astype(BF)
    query_scale = contract_cols(head_row, one_hot(places[0:1]))
    key_scale = contract_cols(head_row, one_hot(places[1:2]))
    gains[:, :D] = all_gains
    gains[:, D:] = jnp.concatenate([query_scale, key_scale, jnp.zeros((6, HD), F32)], axis=0)
    rows = tokens[...].astype(F32)
    normed = (rows * inverse_rms(rows) * all_gains[0:1]).astype(BF)
    kept[:, MIXED + 2 * HD :] = normed

    def run(first, second):
        cos, sin = cosine[...], sine[...]
        qk = product(normed, first[:, :768])
        kept_f[...] = qk
        values = product(normed, second[:, :HD]).astype(BF)
        kept[:, VALUES:MIXED] = values

        def prepare(field, scale):
            return rotate(field * inverse_rms(field) * scale, cos, sin).astype(BF)

        k_rot = prepare(qk[:, 2 * HD :], key_scale)
        kept[:, 2 * HD : VALUES] = k_rot
        causal = lax.broadcasted_iota(jnp.int32, (SEQ, SEQ), 1) <= lax.broadcasted_iota(
            jnp.int32, (SEQ, SEQ), 0
        )
        for head in range(2):
            at = slice(head * HD, (head + 1) * HD)
            q_rot = prepare(qk[:, at], query_scale)
            kept[:, at] = q_rot
            scores = jnp.where(causal, contract_cols(q_rot, k_rot) * SCALE, -1e30)
            expo = jnp.exp(scores - jnp.max(scores, axis=-1, keepdims=True))
            probs = expo / jnp.sum(expo, axis=-1, keepdims=True)
            probs_out[head] = probs
            kept[:, MIXED + head * HD : MIXED + (head + 1) * HD] = product(probs.astype(BF), values).astype(BF)
        mine = pl.multiple_of(place[1] * HALF, HALF)
        give = pl.multiple_of((1 - place[1]) * HALF, HALF)
        mixed = MIXED + 2 * HD
        branch_mine[...] = contract_cols(kept[pl.ds(mine, HALF), MIXED:mixed], second[:, HD:768])
        branch_give[...] = contract_cols(kept[pl.ds(give, HALF), MIXED:mixed], second[:, HD:768]).astype(BF)

    @pl.when(place[0] == 0)
    def _():
        run(own, theirs)

    @pl.when(place[0] != 0)
    def _():
        run(theirs, own)


def attend_back_kernel(
    place, grad_mine, grad_their, own, theirs, cosine, sine, gains, kept, kept_f, probs,
    grad, kv_out, grad_q_out, normed_mine, normed_give, query_gain_out,
):
    grad[pl.ds(pl.multiple_of(place[1] * HALF, HALF), HALF), :] = grad_mine[...]
    grad[pl.ds(pl.multiple_of((1 - place[1]) * HALF, HALF), HALF), :] = grad_their[...]

    def run(first, second):
        cos, sin = cosine[...], sine[...]
        query_scale = gains[0:1, D:]
        grad_mixed = product(grad[...], second[:, HD:768]).astype(BF)
        k_rot = kept[:, 2 * HD : VALUES]
        low_values = kept[:, VALUES:MIXED]
        grad_k = jnp.zeros((SEQ, HD), F32)
        grad_v = jnp.zeros((SEQ, HD), F32)
        gain = jnp.zeros((1, HD), F32)
        for head in range(2):
            at = slice(head * HD, (head + 1) * HD)
            weights = probs[head]
            back = grad_mixed[:, at]
            grad_probs = contract_cols(back, low_values)
            center = jnp.sum(weights * grad_probs, axis=-1, keepdims=True)
            grad_scores = (weights * (grad_probs - center)).astype(BF)
            grad_k = grad_k + contract_rows(grad_scores, kept[:, at])
            grad_v = grad_v + contract_rows(weights.astype(BF), back)
            grad_rot = product(grad_scores, k_rot) * SCALE
            field = kept_f[:, at]
            grad_field, terms = norm_back(
                rotate(grad_rot, cos, -sin), field, inverse_rms(field), query_scale
            )
            gain = gain + jnp.sum(terms, axis=0, keepdims=True)
            grad_q_out[:, at] = grad_field.astype(BF)
        kv_out[:, :HD] = (grad_k * SCALE).astype(BF)
        kv_out[:, HD:] = grad_v.astype(BF)
        query_gain_out[...] = jnp.broadcast_to(gain, (8, HD))
        mine = pl.multiple_of(place[1] * HALF, HALF)
        give = pl.multiple_of((1 - place[1]) * HALF, HALF)
        normed_mine[...] = contract_cols(grad_q_out[pl.ds(mine, HALF), :], first[:, : 2 * HD])
        normed_give[...] = contract_cols(grad_q_out[pl.ds(give, HALF), :], first[:, : 2 * HD]).astype(BF)

    @pl.when(place[0] == 0)
    def _():
        run(own, theirs)

    @pl.when(place[0] != 0)
    def _():
        run(theirs, own)


def input_kernel(
    place, tokens, grad_hidden, own, theirs, places, cosine, sine, gains, kept_f,
    kv_own, kv_their, part_mine, part_their, query_gain, half_gains,
    input_half, grad_kv, gain_rows,
):
    kv = kv_own[...].astype(F32) + kv_their[...].astype(F32)
    keys = kept_f[:, 2 * HD :]
    grad_keys, key_terms = norm_back(
        rotate(kv[:, :HD], cosine[...], -sine[...]), keys, inverse_rms(keys), gains[1:2, D:]
    )
    key_gain = 0.5 * jnp.sum(key_terms, axis=0, keepdims=True)
    grad_kv[:, :HD] = grad_keys.astype(BF)
    grad_kv[:, HD:] = kv[:, HD:].astype(BF)
    low = jnp.concatenate([query_gain[0:1], key_gain], axis=1)
    high = low.astype(BF)
    rest = (low - high.astype(F32)).astype(BF)

    def spread(part):
        return product(part[:, :HD], one_hot(places[0:1])) + product(part[:, HD:], one_hot(places[1:2]))

    head_row = spread(high) + spread(rest)
    mine = pl.multiple_of(place[1] * HALF, HALF)

    def run(first, second):
        grad_normed = (
            part_mine[...]
            + part_their[...].astype(F32)
            + contract_cols(grad_kv[pl.ds(mine, HALF), :HD], first[:, 2 * HD : 768])
            + contract_cols(grad_kv[pl.ds(mine, HALF), HD:], second[:, :HD])
        )
        rows = tokens[pl.ds(mine, HALF), :].astype(F32)
        add, terms = norm_back(grad_normed, rows, inverse_rms(rows), gains[0:1, :D])
        input_half[...] = grad_hidden[...] + add
        input_gain = jnp.sum(terms, axis=0, keepdims=True)
        gain_rows[...] = jnp.concatenate(
            [input_gain, half_gains[0:3], head_row, jnp.zeros((3, D), F32)], axis=0
        )

    @pl.when(place[0] == 0)
    def _():
        run(own, theirs)

    @pl.when(place[0] != 0)
    def _():
        run(theirs, own)


def weights_kernel(place, kept, grad_q, grad_kv, grad_branch, keep, give):
    normed = kept[:, MIXED + 2 * HD :]

    def run(side0, side1):
        side0[:, : 2 * HD] = contract_rows(normed, grad_q[...]).astype(BF)
        side0[:, 2 * HD :] = contract_rows(normed, grad_kv[:, :HD]).astype(BF)
        side1[:, :HD] = contract_rows(normed, grad_kv[:, HD:]).astype(BF)
        side1[:, HD:] = contract_rows(grad_branch[...], kept[:, MIXED : MIXED + 2 * HD]).astype(BF)

    @pl.when(place[0] == 0)
    def _():
        run(keep, give)

    @pl.when(place[0] != 0)
    def _():
        run(give, keep)


def assemble_kernel(keep, their, gains0, gains1, gains2, gains3, out):
    out[:, :768] = (keep[...].astype(F32) + their[...].astype(F32)).astype(BF)
    sums = (gains0[...] + gains1[...]) + (gains2[...] + gains3[...])
    out[:, 768:] = contract_rows(sums.astype(BF), corner()).astype(BF)


TILES = ((0, 256), (256, 512), (512, 768), (768, 896))
ROOT = np.float32(np.sqrt(2.0 / np.pi))


def feed_kernel(*refs):
    count = len(refs) - 7
    pieces, (weights, mine, give, activ_out, gelu_out, slope_out, hold) = refs[:count], refs[count:]
    at = 0
    for piece in pieces:
        hold[at : at + piece.shape[0], :] = piece[...]
        at += piece.shape[0]
    half = at // 2
    for base, out in ((0, mine), (half, give)):
        part = slice(base, base + half)
        block = hold[part, :]
        for low, high in TILES:
            gate = product(block, weights[:, low:high])
            upper = product(block, weights[:, PAD + low : PAD + high])
            square = gate * gate
            tanh = jnp.tanh(ROOT * gate * (1.0 + 0.044715 * square))
            rise = 0.5 * (1.0 + tanh)
            gelu = gate * rise
            slope = rise + 0.5 * gate * (1.0 - tanh * tanh) * (ROOT * (1.0 + 3 * 0.044715 * square))
            gelu_out[part, low:high] = gelu.astype(BF)
            slope_out[part, low:high] = (upper * slope).astype(BF)
            activ_out[part, low:high] = (gelu * upper).astype(BF)
        out[...] = contract_cols(activ_out[part, :], weights[:, 2 * PAD :]).astype(out.dtype)


def feed_back_kernel(*refs):
    count = len(refs) - 7
    pieces, (weights, gelu, slope, mine, give, both, hold) = refs[:count], refs[count:]
    at = 0
    for piece in pieces:
        hold[at : at + piece.shape[0], :] = piece[...]
        at += piece.shape[0]
    half = at // 2
    for base, out in ((0, mine), (half, give)):
        part = slice(base, base + half)
        block = hold[part, :]
        for low, high in TILES:
            grad = product(block, weights[:, 2 * PAD + low : 2 * PAD + high])
            both[part, low:high] = (grad * slope[part, low:high].astype(F32)).astype(BF)
            both[part, PAD + low : PAD + high] = (grad * gelu[part, low:high].astype(F32)).astype(BF)
        out[...] = contract_cols(both[part, :], weights[:, : 2 * PAD]).astype(out.dtype)


def feed_weights_kernel(
    f0, f1, f2, f3, f4, f5, g0, g1, g2, g3, g4, g5, both0, both1, activ0, activ1, out, turned, right
):
    for parts, sides, start, width in (
        ((f0, f1, f2, f3, f4, f5), (both0, both1), 0, 2 * PAD),
        ((g0, g1, g2, g3, g4, g5), (activ0, activ1), 2 * PAD, PAD),
    ):
        at = 0
        for piece in parts:
            turned[:, at : at + piece.shape[0]] = piece[...].T
            at += piece.shape[0]
        right[: 2 * HALF, :width] = sides[0][...]
        right[2 * HALF :, :width] = sides[1][...]
        for low in range(0, width, 256):
            high = min(low + 256, width)
            out[:, start + low : start + high] = product(turned[...], right[:, low:high]).astype(BF)


def local(kernel, outs, count, flops, flagged=True, scratch=()):
    shapes = [jax.ShapeDtypeStruct(shape, dtype) for shape, dtype in outs]
    return pl.pallas_call(
        kernel,
        out_shape=shapes,
        in_specs=[pl.BlockSpec(memory_space=pltpu.SMEM)] * flagged
        + [pl.BlockSpec(memory_space=pltpu.VMEM)] * count,
        out_specs=[pl.BlockSpec(memory_space=pltpu.VMEM)] * len(outs),
        scratch_shapes=[pltpu.VMEM(shape, BF) for shape in scratch],
        compiler_params=pltpu.CompilerParams(vmem_limit_bytes=48 * 2**20),
        cost_estimate=pl.CostEstimate(flops=flops, bytes_accessed=8 * 2**20, transcendentals=200000),
    )


def feed_forward(pieces, weights):
    rows = sum(piece.shape[0] for piece in pieces)
    units = ((rows, PAD), BF)
    return local(
        feed_kernel,
        [((rows // 2, D), F32), ((rows // 2, D), BF), units, units, units],
        len(pieces) + 1,
        rows * 6300000,
        False,
        ((rows, D),),
    )(*pieces, weights)


def feed_backward(pieces, weights, past):
    rows = sum(piece.shape[0] for piece in pieces)
    return local(
        feed_back_kernel,
        [((rows // 2, D), F32), ((rows // 2, D), BF), ((rows, 2 * PAD), BF)],
        len(pieces) + 3,
        rows * 6300000,
        False,
        ((rows, D),),
    )(*pieces, weights, past[3], past[4])


def column_cut(blocks, place):
    pieces = []
    for mask in range(4):
        block = lax.dynamic_index_in_dim(blocks, place ^ mask, 0, keepdims=False)
        pieces.append(block if mask == 0 else swap(block, ("zl", "c"), mask, 4))
    arrived = jnp.stack(pieces)
    return jnp.stack([lax.dynamic_index_in_dim(arrived, place ^ k, 0, keepdims=False) for k in range(4)])


def quarters(weight):
    cut = weight.reshape(weight.shape[0], 4, UNITS).transpose(1, 0, 2)
    return jnp.pad(cut, ((0, 0), (0, 0), (0, PAD - UNITS)))


def whole_units(block):
    return block[:, :, :UNITS].transpose(1, 0, 2).reshape(block.shape[1], 4 * UNITS)


def on_device(
    tokens,
    cotangent,
    input_gain,
    query_weight,
    key_weight,
    value_weight,
    query_gain,
    key_gain,
    output_weight,
    attention_gain,
    feed_gain,
    gate_weight,
    up_weight,
    down_weight,
    output_gain,
):
    core = lax.axis_index("c")
    member = lax.axis_index("t")
    shard = input_gain.shape[0]
    heads_gain = jnp.concatenate([query_gain, key_gain, jnp.zeros((shard - 8,), BF)])
    gains = jnp.stack([input_gain, attention_gain, feed_gain, output_gain, heads_gain], axis=1)
    gains = jnp.pad(gains, ((0, 0), (0, 123)))
    half0 = jnp.concatenate([query_weight, key_weight, gains], axis=1)
    half1 = jnp.concatenate([value_weight, output_weight.T, gains], axis=1)
    column = 2 * lax.axis_index("zl") + core
    att_pack = jnp.stack([half0, half1, half0, half1])
    att_shard = lax.all_to_all(att_pack, ("zl", "c"), 0, 0, tiled=True).reshape(4 * shard, PAD)
    ffn_pack = jnp.concatenate(
        [quarters(gate_weight), quarters(up_weight), quarters(down_weight.T)], axis=2
    )
    ffn_shard = column_cut(ffn_pack, column).reshape(4 * shard, 3 * PAD)
    att_half = lax.all_to_all(
        jnp.broadcast_to(att_shard[None], (16, *att_shard.shape)), PLANE, 0, 0, tiled=True
    ).reshape(D, PAD)
    feed_weights = lax.all_gather(ffn_shard, PLANE, axis=0, tiled=True)

    flag = jnp.stack([core, member]).astype(jnp.int32)
    their_half = other_core(att_half)
    cosine, sine = tables()
    places = head_places()
    gains, kept, kept_f, probs_f, branch_mine, branch_give = local(
        attend_kernel,
        [
            ((8, D + HD), F32), ((SEQ, MIXED + 2 * HD + D), BF), ((SEQ, 768), F32), ((2, SEQ, SEQ), F32),
            ((HALF, D), F32), ((HALF, D), BF),
        ],
        6,
        1100000000,
    )(flag, tokens, att_half, their_half, places, cosine, sine)
    post_gain, feed_scale, final_gain = (gains[i : i + 1, :D] for i in (1, 2, 3))

    def my_half(field):
        return lax.dynamic_slice_in_dim(field, member * HALF, HALF, 0)

    def whole_rows(field):
        theirs = other_member(field)
        top = jnp.where(member == 0, field, theirs)
        bottom = jnp.where(member == 0, theirs, field)
        return jnp.concatenate([top, bottom], axis=0)

    branch = branch_mine + other_member(branch_give).astype(F32)
    my_rows = my_half(tokens).astype(F32)
    inv_b = inverse_rms(branch)
    hidden = my_rows + branch * inv_b * post_gain
    inv_h = inverse_rms(hidden)
    feed = (hidden * inv_h * feed_scale).astype(BF)

    feeds = gathered(feed)
    saved = [feed_forward(pieces, feed_weights) for pieces in feeds]
    second = summed(saved[0], saved[1])
    inv_s = inverse_rms(second)
    layer_half = (hidden + second * inv_s * final_gain).astype(BF)
    layer_out = whole_rows(layer_half)

    upstream = my_half(cotangent).astype(F32)
    grad_second, final_terms = norm_back(upstream, second, inv_s, final_gain)
    grads = gathered(grad_second.astype(BF))
    backs = [feed_backward(pieces, feed_weights, past) for pieces, past in zip(grads, saved)]
    feed_back = summed(backs[0], backs[1])
    (ffn_grads,) = local(
        feed_weights_kernel,
        [((D, 3 * PAD), BF)],
        16,
        6300000000,
        False,
        ((D, 8 * HALF), (8 * HALF, 2 * PAD)),
    )(*feeds[0], *feeds[1], *grads[0], *grads[1], backs[0][2], backs[1][2], saved[0][2], saved[1][2])
    ffn_sums = lax.psum_scatter(ffn_grads, PLANE, scatter_dimension=0, tiled=True)
    hidden_add, feed_terms = norm_back(feed_back, hidden, inv_h, feed_scale)
    grad_hidden = upstream + hidden_add
    grad_branch, post_terms = norm_back(grad_hidden, branch, inv_b, post_gain)
    grad_mine = grad_branch.astype(BF)
    half_gains = jnp.stack([jnp.sum(terms, axis=0) for terms in (post_terms, feed_terms, final_terms)])
    half_gains = jnp.pad(half_gains, ((0, 5), (0, 0)))

    grad_branch, kv_part, grad_q, normed_mine, normed_give, query_gain = local(
        attend_back_kernel,
        [
            ((SEQ, D), BF), ((SEQ, 2 * HD), BF), ((SEQ, 2 * HD), BF), ((HALF, D), F32), ((HALF, D), BF),
            ((8, HD), F32),
        ],
        10,
        1100000000,
    )(flag, grad_mine, other_member(grad_mine), att_half, their_half, cosine, sine, gains, kept, kept_f, probs_f)
    input_half, grad_kv, gain_rows = local(
        input_kernel,
        [((HALF, D), F32), ((SEQ, 2 * HD), BF), ((8, D), F32)],
        15,
        400000000,
    )(
        flag, tokens, grad_hidden, att_half, their_half, places, cosine, sine, gains, kept_f,
        kv_part, other_member(kv_part), normed_mine, other_member(normed_give), query_gain, half_gains,
    )
    keep, give = local(weights_kernel, [((D, 768), BF), ((D, 768), BF)], 4, 900000000)(
        flag, kept, grad_q, grad_kv, grad_branch
    )
    (att_sums,) = local(assemble_kernel, [((D, PAD), BF)], 6, 10000000, False)(
        keep,
        other_core(give),
        gain_rows,
        *(swap(gain_rows, ("c", "t"), mask, 4) for mask in (2, 1, 3)),
    )
    blocks = ffn_sums.reshape(4, shard, 3 * PAD)
    blocks, att_sums = lax.optimization_barrier((blocks, att_sums))
    ffn_sums = column_cut(blocks, column).astype(F32)
    grad_gate_weight = whole_units(ffn_sums[:, :, :PAD])
    grad_up_weight = whole_units(ffn_sums[:, :, PAD : 2 * PAD])
    grad_down = whole_units(ffn_sums[:, :, 2 * PAD :]).T
    input_grad = whole_rows(input_half)
    att_sums = lax.all_to_all(att_sums.reshape(16, 4 * shard, PAD), PLANE, 0, 0, tiled=True)
    att_sums = jnp.sum(att_sums.astype(F32), axis=0).astype(BF)
    att_sums = lax.all_to_all(att_sums.reshape(4, shard, PAD), ("zl", "c"), 0, 0, tiled=True).astype(F32)
    out0 = att_sums[0] + att_sums[2]
    out1 = att_sums[1] + att_sums[3]

    return (
        layer_out,
        input_grad,
        out0[:, 768],
        out0[:, :512],
        out0[:, 512:768],
        out1[:, :256],
        out0[:4, 772],
        out0[4:8, 772],
        out1[:, 256:768].T,
        out0[:, 769],
        out0[:, 770],
        grad_gate_weight,
        grad_up_weight,
        grad_down,
        out0[:, 771],
    )


def solution(mesh):
    fine = Mesh(mesh.devices.reshape(4, 4, 2, 2, 2), ("y", "x", "zl", "c", "t"))
    dp = ("y", "x", "zl", "c")
    in_specs = (
        P(dp, None),
        P(dp, None),
        P(dp),
        P(dp, "t"),
        P(dp, None),
        P(dp, None),
        P(dp),
        P(dp),
        P("t", dp),
        P(dp),
        P(dp),
        P(dp, "t"),
        P(dp, "t"),
        P("t", dp),
        P(dp),
    )
    out_specs = (
        P(dp, None),
        P(dp, None),
        P(dp),
        P(dp, "t"),
        P(dp, None),
        P(dp, None),
        P(dp),
        P(dp),
        P("t", dp),
        P(dp),
        P(dp),
        P(dp, "t"),
        P(dp, "t"),
        P("t", dp),
        P(dp),
    )
    return jax.shard_map(
        on_device, mesh=fine, in_specs=in_specs, out_specs=out_specs, check_vma=False
    )
```

```python
import jax
import jax.numpy as jnp
import numpy as np
from jax import lax
from jax.experimental import pallas as pl
from jax.experimental.pallas import tpu as pltpu
from jax.sharding import Mesh, PartitionSpec as P

D = 1152
HD = 256
SEQ = 256
HALF = SEQ // 2
UNITS = 864
VALUES = 768
MIXED = 1024
PAD = 896
EPS = 1e-06
THETA = 1000000.0
SCALE = HD ** (-0.5)
BF = jnp.bfloat16
F32 = jnp.float32
PLANE = ("y", "x")


def swap(field, axes, mask, size):
    return lax.ppermute(field, axes, [(i, i ^ mask) for i in range(size)])


def across(field, mask):
    return swap(field, ("zl", "t"), mask, 4)


def other_core(field):
    return swap(field, "c", 1, 2)


def other_member(field):
    return swap(field, "t", 1, 2)


def near_and_far(block, run):
    near = (block, other_core(block))
    far = [across(block, m) for m in (1, 2, 3)]
    first, *rest = run(0, near)
    first, *far = lax.optimization_barrier((first, *far))
    far = (*far, other_core(jnp.concatenate(far, axis=0)))
    return (*near, *far), [(first, *rest), run(1, far)]


def core_sum(far):
    return (far[0] + other_core(far[1]).astype(F32)).astype(BF)


def summed(near, mine):
    far = [across(mine[(m - 1) * HALF : m * HALF], m) for m in (1, 2, 3)]
    total = near[0] + other_core(near[1]).astype(F32)
    for field in far:
        total = total + field.astype(F32)
    return total


def product(left, right):
    return jnp.dot(left, right, preferred_element_type=F32)


def contract_rows(left, right):
    return lax.dot_general(left, right, (((0,), (0,)), ((), ())), preferred_element_type=F32)


def contract_cols(left, right):
    return lax.dot_general(left, right, (((1,), (1,)), ((), ())), preferred_element_type=F32)


def inverse_rms(field):
    return lax.rsqrt(jnp.mean(field * field, axis=-1, keepdims=True) + EPS)


def norm_back(grad, field, inv, gain):
    scaled = grad * gain
    back = inv * scaled - field * (inv * inv * inv) * jnp.mean(field * scaled, axis=-1, keepdims=True)
    return back, grad * field * inv


def tables():
    half = HD // 2
    freq = np.float32(THETA) ** (-np.arange(half, dtype=np.float32) / np.float32(half))
    angle = np.arange(SEQ, dtype=np.float32)[:, None] * freq[None, :].astype(np.float32)
    return jnp.asarray(np.cos(angle).astype(np.float32)), jnp.asarray(np.sin(angle).astype(np.float32))


def rotate(field, cosine, sine):
    half = HD // 2
    first, second = field[..., :half], field[..., half:]
    return jnp.concatenate([first * cosine - second * sine, second * cosine + first * sine], axis=-1)


def head_places():
    place = np.full((2, D), -1, np.int32)
    for row in range(D):
        group, at = divmod(row, 18)
        if at < 8:
            place[at // 4, row] = 4 * group + at % 4
    return jnp.asarray(np.concatenate([place, np.zeros((6, D), np.int32)]))


def one_hot(place_row):
    rows = lax.broadcasted_iota(jnp.int32, (HD, D), 0)
    return jnp.where(rows == place_row, 1.0, 0.0).astype(BF)


def corner():
    rows = lax.broadcasted_iota(jnp.int32, (8, 128), 0)
    return jnp.where(rows == lax.broadcasted_iota(jnp.int32, (8, 128), 1), 1.0, 0.0).astype(BF)


def attend_kernel(
    place, tokens, own, theirs, places, cosine, sine,
    gains, kept, kept_f, probs_out, branch_mine, branch_give,
):
    all_gains = contract_cols(corner(), own[:, 768:])
    head_row = all_gains[4:5].astype(BF)
    query_scale = contract_cols(head_row, one_hot(places[0:1]))
    key_scale = contract_cols(head_row, one_hot(places[1:2]))
    gains[:, :D] = all_gains
    gains[:, D:] = jnp.concatenate([query_scale, key_scale, jnp.zeros((6, HD), F32)], axis=0)
    rows = tokens[...].astype(F32)
    normed = (rows * inverse_rms(rows) * all_gains[0:1]).astype(BF)
    kept[:, MIXED + 2 * HD :] = normed

    def run(first, second):
        cos, sin = cosine[...], sine[...]
        qk = product(normed, first[:, :768])
        kept_f[...] = qk
        values = product(normed, second[:, :HD]).astype(BF)
        kept[:, VALUES:MIXED] = values

        def prepare(field, scale):
            return rotate(field * inverse_rms(field) * scale, cos, sin).astype(BF)

        k_rot = prepare(qk[:, 2 * HD :], key_scale)
        kept[:, 2 * HD : VALUES] = k_rot
        causal = lax.broadcasted_iota(jnp.int32, (SEQ, SEQ), 1) <= lax.broadcasted_iota(
            jnp.int32, (SEQ, SEQ), 0
        )
        for head in range(2):
            at = slice(head * HD, (head + 1) * HD)
            q_rot = prepare(qk[:, at], query_scale)
            kept[:, at] = q_rot
            scores = jnp.where(causal, contract_cols(q_rot, k_rot) * SCALE, -1e30)
            expo = jnp.exp(scores - jnp.max(scores, axis=-1, keepdims=True))
            probs = expo / jnp.sum(expo, axis=-1, keepdims=True)
            probs_out[head] = probs
            kept[:, MIXED + head * HD : MIXED + (head + 1) * HD] = product(probs.astype(BF), values).astype(BF)
        mine = pl.multiple_of(place[1] * HALF, HALF)
        give = pl.multiple_of((1 - place[1]) * HALF, HALF)
        mixed = MIXED + 2 * HD
        branch_mine[...] = contract_cols(kept[pl.ds(mine, HALF), MIXED:mixed], second[:, HD:768])
        branch_give[...] = contract_cols(kept[pl.ds(give, HALF), MIXED:mixed], second[:, HD:768]).astype(BF)

    @pl.when(place[0] == 0)
    def _():
        run(own, theirs)

    @pl.when(place[0] != 0)
    def _():
        run(theirs, own)


def attend_back_kernel(
    place, grad_mine, grad_their, own, theirs, cosine, sine, gains, kept, kept_f, probs,
    grad, kv_out, grad_q_out, normed_mine, normed_give, query_gain_out,
):
    grad[pl.ds(pl.multiple_of(place[1] * HALF, HALF), HALF), :] = grad_mine[...]
    grad[pl.ds(pl.multiple_of((1 - place[1]) * HALF, HALF), HALF), :] = grad_their[...]

    def run(first, second):
        cos, sin = cosine[...], sine[...]
        query_scale = gains[0:1, D:]
        grad_mixed = product(grad[...], second[:, HD:768]).astype(BF)
        k_rot = kept[:, 2 * HD : VALUES]
        low_values = kept[:, VALUES:MIXED]
        grad_k = jnp.zeros((SEQ, HD), F32)
        grad_v = jnp.zeros((SEQ, HD), F32)
        gain = jnp.zeros((1, HD), F32)
        for head in range(2):
            at = slice(head * HD, (head + 1) * HD)
            weights = probs[head]
            back = grad_mixed[:, at]
            grad_probs = contract_cols(back, low_values)
            center = jnp.sum(weights * grad_probs, axis=-1, keepdims=True)
            grad_scores = (weights * (grad_probs - center)).astype(BF)
            grad_k = grad_k + contract_rows(grad_scores, kept[:, at])
            grad_v = grad_v + contract_rows(weights.astype(BF), back)
            grad_rot = product(grad_scores, k_rot) * SCALE
            field = kept_f[:, at]
            grad_field, terms = norm_back(
                rotate(grad_rot, cos, -sin), field, inverse_rms(field), query_scale
            )
            gain = gain + jnp.sum(terms, axis=0, keepdims=True)
            grad_q_out[:, at] = grad_field.astype(BF)
        kv_out[:, :HD] = (grad_k * SCALE).astype(BF)
        kv_out[:, HD:] = grad_v.astype(BF)
        query_gain_out[...] = jnp.broadcast_to(gain, (8, HD))
        mine = pl.multiple_of(place[1] * HALF, HALF)
        give = pl.multiple_of((1 - place[1]) * HALF, HALF)
        normed_mine[...] = contract_cols(grad_q_out[pl.ds(mine, HALF), :], first[:, : 2 * HD])
        normed_give[...] = contract_cols(grad_q_out[pl.ds(give, HALF), :], first[:, : 2 * HD]).astype(BF)

    @pl.when(place[0] == 0)
    def _():
        run(own, theirs)

    @pl.when(place[0] != 0)
    def _():
        run(theirs, own)


def input_kernel(
    place, tokens, grad_hidden, own, theirs, places, cosine, sine, gains, kept_f,
    kv_own, kv_their, part_mine, part_their, query_gain, half_gains,
    input_half, grad_kv, gain_rows,
):
    kv = kv_own[...].astype(F32) + kv_their[...].astype(F32)
    keys = kept_f[:, 2 * HD :]
    grad_keys, key_terms = norm_back(
        rotate(kv[:, :HD], cosine[...], -sine[...]), keys, inverse_rms(keys), gains[1:2, D:]
    )
    key_gain = 0.5 * jnp.sum(key_terms, axis=0, keepdims=True)
    grad_kv[:, :HD] = grad_keys.astype(BF)
    grad_kv[:, HD:] = kv[:, HD:].astype(BF)
    low = jnp.concatenate([query_gain[0:1], key_gain], axis=1)
    high = low.astype(BF)
    rest = (low - high.astype(F32)).astype(BF)

    def spread(part):
        return product(part[:, :HD], one_hot(places[0:1])) + product(part[:, HD:], one_hot(places[1:2]))

    head_row = spread(high) + spread(rest)
    mine = pl.multiple_of(place[1] * HALF, HALF)

    def run(first, second):
        grad_normed = (
            part_mine[...]
            + part_their[...].astype(F32)
            + contract_cols(grad_kv[pl.ds(mine, HALF), :HD], first[:, 2 * HD : 768])
            + contract_cols(grad_kv[pl.ds(mine, HALF), HD:], second[:, :HD])
        )
        rows = tokens[pl.ds(mine, HALF), :].astype(F32)
        add, terms = norm_back(grad_normed, rows, inverse_rms(rows), gains[0:1, :D])
        input_half[...] = grad_hidden[...] + add
        input_gain = jnp.sum(terms, axis=0, keepdims=True)
        gain_rows[...] = jnp.concatenate(
            [input_gain, half_gains[0:3], head_row, jnp.zeros((3, D), F32)], axis=0
        )

    @pl.when(place[0] == 0)
    def _():
        run(own, theirs)

    @pl.when(place[0] != 0)
    def _():
        run(theirs, own)


def weights_kernel(place, kept, grad_q, grad_kv, grad_branch, keep, give):
    normed = kept[:, MIXED + 2 * HD :]

    def run(side0, side1):
        side0[:, : 2 * HD] = contract_rows(normed, grad_q[...]).astype(BF)
        side0[:, 2 * HD :] = contract_rows(normed, grad_kv[:, :HD]).astype(BF)
        side1[:, :HD] = contract_rows(normed, grad_kv[:, HD:]).astype(BF)
        side1[:, HD:] = contract_rows(grad_branch[...], kept[:, MIXED : MIXED + 2 * HD]).astype(BF)

    @pl.when(place[0] == 0)
    def _():
        run(keep, give)

    @pl.when(place[0] != 0)
    def _():
        run(give, keep)


def assemble_kernel(keep, their, gains0, gains1, gains2, gains3, layer, out, layer_out):
    layer_out[...] = layer[...]
    out[:, :768] = (keep[...].astype(F32) + their[...].astype(F32)).astype(BF)
    sums = (gains0[...] + gains1[...]) + (gains2[...] + gains3[...])
    out[:, 768:] = contract_rows(sums.astype(BF), corner()).astype(BF)


TILES = ((0, 256), (256, 512), (512, 768), (768, 896))
ROOT = np.float32(np.sqrt(2.0 / np.pi))


def feed_kernel(*refs):
    count = len(refs) - 7
    pieces, (weights, mine, give, activ_out, gelu_out, slope_out, hold) = refs[:count], refs[count:]
    at = 0
    for piece in pieces:
        hold[at : at + piece.shape[0], :] = piece[...]
        at += piece.shape[0]
    half = at // 2
    for base, out in ((0, mine), (half, give)):
        part = slice(base, base + half)
        block = hold[part, :]
        for low, high in TILES:
            gate = product(block, weights[:, low:high])
            upper = product(block, weights[:, PAD + low : PAD + high])
            square = gate * gate
            tanh = jnp.tanh(ROOT * gate * (1.0 + 0.044715 * square))
            rise = 0.5 * (1.0 + tanh)
            gelu = gate * rise
            slope = rise + 0.5 * gate * (1.0 - tanh * tanh) * (ROOT * (1.0 + 3 * 0.044715 * square))
            gelu_out[part, low:high] = gelu.astype(BF)
            slope_out[part, low:high] = (upper * slope).astype(BF)
            activ_out[part, low:high] = (gelu * upper).astype(BF)
        out[...] = contract_cols(activ_out[part, :], weights[:, 2 * PAD :]).astype(out.dtype)


def feed_back_kernel(*refs):
    count = len(refs) - 7
    pieces, (weights, gelu, slope, mine, give, both, hold) = refs[:count], refs[count:]
    at = 0
    for piece in pieces:
        hold[at : at + piece.shape[0], :] = piece[...]
        at += piece.shape[0]
    half = at // 2
    for base, out in ((0, mine), (half, give)):
        part = slice(base, base + half)
        block = hold[part, :]
        for low, high in TILES:
            grad = product(block, weights[:, 2 * PAD + low : 2 * PAD + high])
            both[part, low:high] = (grad * slope[part, low:high].astype(F32)).astype(BF)
            both[part, PAD + low : PAD + high] = (grad * gelu[part, low:high].astype(F32)).astype(BF)
        out[...] = contract_cols(both[part, :], weights[:, : 2 * PAD]).astype(out.dtype)


def feed_weights_kernel(
    f0, f1, f2, f3, f4, f5, g0, g1, g2, g3, g4, g5, both0, both1, activ0, activ1, out, turned, right
):
    for parts, sides, start, width in (
        ((f0, f1, f2, f3, f4, f5), (both0, both1), 0, 2 * PAD),
        ((g0, g1, g2, g3, g4, g5), (activ0, activ1), 2 * PAD, PAD),
    ):
        at = 0
        for piece in parts:
            turned[:, at : at + piece.shape[0]] = piece[...].T
            at += piece.shape[0]
        right[: 2 * HALF, :width] = sides[0][...]
        right[2 * HALF :, :width] = sides[1][...]
        for low in range(0, width, 256):
            high = min(low + 256, width)
            out[:, start + low : start + high] = product(turned[...], right[:, low:high]).astype(BF)


def local(kernel, outs, count, flops, flagged=True, scratch=(), room=16):
    shapes = [jax.ShapeDtypeStruct(shape, dtype) for shape, dtype in outs]
    return pl.pallas_call(
        kernel,
        out_shape=shapes,
        in_specs=[pl.BlockSpec(memory_space=pltpu.SMEM)] * flagged
        + [pl.BlockSpec(memory_space=pltpu.VMEM)] * count,
        out_specs=[pl.BlockSpec(memory_space=pltpu.VMEM)] * len(outs),
        scratch_shapes=[pltpu.VMEM(shape, BF) for shape in scratch],
        compiler_params=pltpu.CompilerParams(vmem_limit_bytes=room * 2**20),
        cost_estimate=pl.CostEstimate(flops=flops, bytes_accessed=8 * 2**20, transcendentals=200000),
    )


def feed_forward(pieces, weights):
    rows = sum(piece.shape[0] for piece in pieces)
    units = ((rows, PAD), BF)
    return local(
        feed_kernel,
        [((rows // 2, D), F32), ((rows // 2, D), BF), units, units, units],
        len(pieces) + 1,
        rows * 6300000,
        False,
        ((rows, D),),
        24,
    )(*pieces, weights)


def feed_backward(pieces, weights, past):
    rows = sum(piece.shape[0] for piece in pieces)
    return local(
        feed_back_kernel,
        [((rows // 2, D), F32), ((rows // 2, D), BF), ((rows, 2 * PAD), BF)],
        len(pieces) + 3,
        rows * 6300000,
        False,
        ((rows, D),),
        24,
    )(*pieces, weights, past[3], past[4])


def column_cut(blocks, place):
    pieces = []
    for mask in range(4):
        block = lax.dynamic_index_in_dim(blocks, place ^ mask, 0, keepdims=False)
        pieces.append(block if mask == 0 else swap(block, ("zl", "c"), mask, 4))
    arrived = jnp.stack(pieces)
    return jnp.stack([lax.dynamic_index_in_dim(arrived, place ^ k, 0, keepdims=False) for k in range(4)])


def quarters(weight):
    cut = weight.reshape(weight.shape[0], 4, UNITS).transpose(1, 0, 2)
    return jnp.pad(cut, ((0, 0), (0, 0), (0, PAD - UNITS)))


def whole_units(block):
    return block[:, :, :UNITS].transpose(1, 0, 2).reshape(block.shape[1], 4 * UNITS)


def on_device(
    tokens,
    cotangent,
    input_gain,
    query_weight,
    key_weight,
    value_weight,
    query_gain,
    key_gain,
    output_weight,
    attention_gain,
    feed_gain,
    gate_weight,
    up_weight,
    down_weight,
    output_gain,
):
    core = lax.axis_index("c")
    member = lax.axis_index("t")
    shard = input_gain.shape[0]
    heads_gain = jnp.concatenate([query_gain, key_gain, jnp.zeros((shard - 8,), BF)])
    gains = jnp.stack([input_gain, attention_gain, feed_gain, output_gain, heads_gain], axis=1)
    gains = jnp.pad(gains, ((0, 0), (0, 123)))
    half0 = jnp.concatenate([query_weight, key_weight, gains], axis=1)
    half1 = jnp.concatenate([value_weight, output_weight.T, gains], axis=1)
    column = 2 * lax.axis_index("zl") + core
    att_pack = jnp.stack([half0, half1, half0, half1])
    att_shard = lax.all_to_all(att_pack, ("zl", "c"), 0, 0, tiled=True).reshape(4 * shard, PAD)
    att_shard, gate_weight, up_weight, down_weight = lax.optimization_barrier(
        (att_shard, gate_weight, up_weight, down_weight)
    )
    ffn_pack = jnp.concatenate(
        [quarters(gate_weight), quarters(up_weight), quarters(down_weight.T)], axis=2
    )
    ffn_shard = column_cut(ffn_pack, column).reshape(4 * shard, 3 * PAD)
    att_half = lax.all_to_all(
        jnp.broadcast_to(att_shard[None], (16, *att_shard.shape)), PLANE, 0, 0, tiled=True
    ).reshape(D, PAD)
    feed_weights = lax.all_gather(ffn_shard, PLANE, axis=0, tiled=True)

    flag = jnp.stack([core, member]).astype(jnp.int32)
    their_half = other_core(att_half)
    cosine, sine = tables()
    places = head_places()
    gains, kept, kept_f, probs_f, branch_mine, branch_give = local(
        attend_kernel,
        [
            ((8, D + HD), F32), ((SEQ, MIXED + 2 * HD + D), BF), ((SEQ, 768), F32), ((2, SEQ, SEQ), F32),
            ((HALF, D), F32), ((HALF, D), BF),
        ],
        6,
        1100000000,
    )(flag, tokens, att_half, their_half, places, cosine, sine)
    post_gain, feed_scale, final_gain = (gains[i : i + 1, :D] for i in (1, 2, 3))

    def my_half(field):
        return lax.dynamic_slice_in_dim(field, member * HALF, HALF, 0)

    def whole_rows(field, theirs):
        top = jnp.where(member == 0, field, theirs)
        bottom = jnp.where(member == 0, theirs, field)
        return jnp.concatenate([top, bottom], axis=0)

    branch = branch_mine + other_member(branch_give).astype(F32)
    my_rows = my_half(tokens).astype(F32)
    inv_b = inverse_rms(branch)
    hidden = my_rows + branch * inv_b * post_gain
    inv_h = inverse_rms(hidden)
    feed = (hidden * inv_h * feed_scale).astype(BF)

    feeds, saved = near_and_far(feed, lambda _, pieces: feed_forward(pieces, feed_weights))
    second = summed(saved[0], core_sum(saved[1]))
    inv_s = inverse_rms(second)
    layer_half = (hidden + second * inv_s * final_gain).astype(BF)

    upstream = my_half(cotangent).astype(F32)
    grad_second, final_terms = norm_back(upstream, second, inv_s, final_gain)
    grads, backs = near_and_far(
        grad_second.astype(BF), lambda i, pieces: feed_backward(pieces, feed_weights, saved[i])
    )
    feed_back = summed(backs[0], core_sum(backs[1]))
    (ffn_grads,) = local(
        feed_weights_kernel,
        [((D, 3 * PAD), BF)],
        16,
        6300000000,
        False,
        ((D, 8 * HALF), (8 * HALF, 2 * PAD)),
        30,
    )(*feeds, *grads, backs[0][2], backs[1][2], saved[0][2], saved[1][2])
    ffn_sums = lax.psum_scatter(ffn_grads, PLANE, scatter_dimension=0, tiled=True)
    hidden_add, feed_terms = norm_back(feed_back, hidden, inv_h, feed_scale)
    grad_hidden = upstream + hidden_add
    grad_branch, post_terms = norm_back(grad_hidden, branch, inv_b, post_gain)
    grad_mine = grad_branch.astype(BF)
    half_gains = jnp.stack([jnp.sum(terms, axis=0) for terms in (post_terms, feed_terms, final_terms)])
    half_gains = jnp.pad(half_gains, ((0, 5), (0, 0)))

    grad_branch, kv_part, grad_q, normed_mine, normed_give, query_gain = local(
        attend_back_kernel,
        [
            ((SEQ, D), BF), ((SEQ, 2 * HD), BF), ((SEQ, 2 * HD), BF), ((HALF, D), F32), ((HALF, D), BF),
            ((8, HD), F32),
        ],
        10,
        1100000000,
    )(flag, grad_mine, other_member(grad_mine), att_half, their_half, cosine, sine, gains, kept, kept_f, probs_f)
    input_half, grad_kv, gain_rows = local(
        input_kernel,
        [((HALF, D), F32), ((SEQ, 2 * HD), BF), ((8, D), F32)],
        15,
        400000000,
    )(
        flag, tokens, grad_hidden, att_half, their_half, places, cosine, sine, gains, kept_f,
        kv_part, other_member(kv_part), normed_mine, other_member(normed_give), query_gain, half_gains,
    )
    keep, give = local(weights_kernel, [((D, 768), BF), ((D, 768), BF)], 4, 900000000)(
        flag, kept, grad_q, grad_kv, grad_branch
    )
    att_sums, layer_half = local(
        assemble_kernel, [((D, PAD), BF), ((HALF, D), BF)], 7, 10000000, False
    )(
        keep,
        other_core(give),
        gain_rows,
        *(swap(gain_rows, ("c", "t"), mask, 4) for mask in (2, 1, 3)),
        layer_half,
    )
    att_sums, input_half = lax.optimization_barrier((att_sums, input_half))
    ffn_sums = column_cut(ffn_sums.reshape(4, shard, 3 * PAD), column)
    input_grad = whole_rows(input_half, other_member(input_half))
    layer_out = whole_rows(layer_half, other_member(layer_half))
    att_sums = lax.all_to_all(att_sums.reshape(16, 4 * shard, PAD), PLANE, 0, 0, tiled=True)
    att_sums = jnp.sum(att_sums.astype(F32), axis=0).astype(BF)
    att_sums, ffn_sums = lax.optimization_barrier((att_sums, ffn_sums))
    ffn_sums = ffn_sums.astype(F32)
    grad_gate_weight = whole_units(ffn_sums[:, :, :PAD])
    grad_up_weight = whole_units(ffn_sums[:, :, PAD : 2 * PAD])
    grad_down = whole_units(ffn_sums[:, :, 2 * PAD :]).T
    att_sums = lax.all_to_all(att_sums.reshape(4, shard, PAD), ("zl", "c"), 0, 0, tiled=True).astype(F32)
    out0 = att_sums[0] + att_sums[2]
    out1 = att_sums[1] + att_sums[3]

    return (
        layer_out,
        input_grad,
        out0[:, 768],
        out0[:, :512],
        out0[:, 512:768],
        out1[:, :256],
        out0[:4, 772],
        out0[4:8, 772],
        out1[:, 256:768].T,
        out0[:, 769],
        out0[:, 770],
        grad_gate_weight,
        grad_up_weight,
        grad_down,
        out0[:, 771],
    )


def solution(mesh):
    fine = Mesh(mesh.devices.reshape(4, 4, 2, 2, 2), ("y", "x", "zl", "c", "t"))
    dp = ("y", "x", "zl", "c")
    in_specs = (
        P(dp, None),
        P(dp, None),
        P(dp),
        P(dp, "t"),
        P(dp, None),
        P(dp, None),
        P(dp),
        P(dp),
        P("t", dp),
        P(dp),
        P(dp),
        P(dp, "t"),
        P(dp, "t"),
        P("t", dp),
        P(dp),
    )
    out_specs = (
        P(dp, None),
        P(dp, None),
        P(dp),
        P(dp, "t"),
        P(dp, None),
        P(dp, None),
        P(dp),
        P(dp),
        P("t", dp),
        P(dp),
        P(dp),
        P(dp, "t"),
        P(dp, "t"),
        P("t", dp),
        P(dp),
    )
    return jax.shard_map(
        on_device, mesh=fine, in_specs=in_specs, out_specs=out_specs, check_vma=False
    )
```

```python
import jax
import jax.numpy as jnp
import numpy as np
from jax import lax
from jax.experimental import pallas as pl
from jax.experimental.pallas import tpu as pltpu
from jax.sharding import Mesh, PartitionSpec as P

D = 1152
HD = 256
SEQ = 256
HALF = SEQ // 2
UNITS = 864
VALUES = 768
MIXED = 1024
PAD = 896
EPS = 1e-06
THETA = 1000000.0
SCALE = HD ** (-0.5)
BF = jnp.bfloat16
F32 = jnp.float32
PLANE = ("y", "x")


def swap(field, axes, mask, size):
    return lax.ppermute(field, axes, [(i, i ^ mask) for i in range(size)])


def across(field, mask):
    return swap(field, ("zl", "t"), mask, 4)


def other_core(field):
    return swap(field, "c", 1, 2)


def other_member(field):
    return swap(field, "t", 1, 2)


def near_and_far(block, run):
    near = (block, other_core(block))
    far = [across(block, m) for m in (1, 2, 3)]
    first, *rest = run(0, near)
    first, *far = lax.optimization_barrier((first, *far))
    far = (*far, other_core(jnp.concatenate(far, axis=0)))
    return (*near, *far), [(first, *rest), run(1, far)]


def core_sum(far):
    return (far[0] + other_core(far[1]).astype(F32)).astype(BF)


def summed(near, mine):
    far = [across(mine[(m - 1) * HALF : m * HALF], m) for m in (1, 2, 3)]
    total = near[0] + other_core(near[1]).astype(F32)
    for field in far:
        total = total + field.astype(F32)
    return total


def product(left, right):
    return jnp.dot(left, right, preferred_element_type=F32)


def contract_rows(left, right):
    return lax.dot_general(left, right, (((0,), (0,)), ((), ())), preferred_element_type=F32)


def contract_cols(left, right):
    return lax.dot_general(left, right, (((1,), (1,)), ((), ())), preferred_element_type=F32)


def inverse_rms(field):
    return lax.rsqrt(jnp.mean(field * field, axis=-1, keepdims=True) + EPS)


def norm_back(grad, field, inv, gain):
    scaled = grad * gain
    back = inv * scaled - field * (inv * inv * inv) * jnp.mean(field * scaled, axis=-1, keepdims=True)
    return back, grad * field * inv


def tables():
    half = HD // 2
    freq = np.float32(THETA) ** (-np.arange(half, dtype=np.float32) / np.float32(half))
    angle = np.arange(SEQ, dtype=np.float32)[:, None] * freq[None, :].astype(np.float32)
    return jnp.asarray(np.cos(angle).astype(np.float32)), jnp.asarray(np.sin(angle).astype(np.float32))


def rotate(field, cosine, sine):
    half = HD // 2
    first, second = field[..., :half], field[..., half:]
    return jnp.concatenate([first * cosine - second * sine, second * cosine + first * sine], axis=-1)


def head_places():
    place = np.full((2, D), -1, np.int32)
    for row in range(D):
        group, at = divmod(row, 18)
        if at < 8:
            place[at // 4, row] = 4 * group + at % 4
    return jnp.asarray(np.concatenate([place, np.zeros((6, D), np.int32)]))


def one_hot(place_row):
    rows = lax.broadcasted_iota(jnp.int32, (HD, D), 0)
    return jnp.where(rows == place_row, 1.0, 0.0).astype(BF)


def corner():
    rows = lax.broadcasted_iota(jnp.int32, (8, 128), 0)
    return jnp.where(rows == lax.broadcasted_iota(jnp.int32, (8, 128), 1), 1.0, 0.0).astype(BF)


def attend_kernel(
    place, tokens, own, theirs, places, cosine, sine,
    gains, kept, kept_f, probs_out, branch_mine, branch_give,
):
    all_gains = contract_cols(corner(), own[:, 768:])
    head_row = all_gains[4:5].astype(BF)
    query_scale = contract_cols(head_row, one_hot(places[0:1]))
    key_scale = contract_cols(head_row, one_hot(places[1:2]))
    gains[:, :D] = all_gains
    gains[:, D:] = jnp.concatenate([query_scale, key_scale, jnp.zeros((6, HD), F32)], axis=0)
    rows = tokens[...].astype(F32)
    normed = (rows * inverse_rms(rows) * all_gains[0:1]).astype(BF)
    kept[:, MIXED + 2 * HD :] = normed

    def run(first, second):
        cos, sin = cosine[...], sine[...]
        qk = product(normed, first[:, :768])
        kept_f[...] = qk
        values = product(normed, second[:, :HD]).astype(BF)
        kept[:, VALUES:MIXED] = values

        def prepare(field, scale):
            return rotate(field * inverse_rms(field) * scale, cos, sin).astype(BF)

        k_rot = prepare(qk[:, 2 * HD :], key_scale)
        kept[:, 2 * HD : VALUES] = k_rot
        causal = lax.broadcasted_iota(jnp.int32, (SEQ, SEQ), 1) <= lax.broadcasted_iota(
            jnp.int32, (SEQ, SEQ), 0
        )
        for head in range(2):
            at = slice(head * HD, (head + 1) * HD)
            q_rot = prepare(qk[:, at], query_scale)
            kept[:, at] = q_rot
            scores = jnp.where(causal, contract_cols(q_rot, k_rot) * SCALE, -1e30)
            expo = jnp.exp(scores - jnp.max(scores, axis=-1, keepdims=True))
            probs = expo / jnp.sum(expo, axis=-1, keepdims=True)
            probs_out[head] = probs
            kept[:, MIXED + head * HD : MIXED + (head + 1) * HD] = product(probs.astype(BF), values).astype(BF)
        mine = pl.multiple_of(place[1] * HALF, HALF)
        give = pl.multiple_of((1 - place[1]) * HALF, HALF)
        mixed = MIXED + 2 * HD
        branch_mine[...] = contract_cols(kept[pl.ds(mine, HALF), MIXED:mixed], second[:, HD:768])
        branch_give[...] = contract_cols(kept[pl.ds(give, HALF), MIXED:mixed], second[:, HD:768]).astype(BF)

    @pl.when(place[0] == 0)
    def _():
        run(own, theirs)

    @pl.when(place[0] != 0)
    def _():
        run(theirs, own)


def attend_back_kernel(
    place, grad_mine, grad_their, own, theirs, cosine, sine, gains, kept, kept_f, probs,
    grad, kv_out, grad_q_out, normed_mine, normed_give, query_gain_out,
):
    grad[pl.ds(pl.multiple_of(place[1] * HALF, HALF), HALF), :] = grad_mine[...]
    grad[pl.ds(pl.multiple_of((1 - place[1]) * HALF, HALF), HALF), :] = grad_their[...]

    def run(first, second):
        cos, sin = cosine[...], sine[...]
        query_scale = gains[0:1, D:]
        grad_mixed = product(grad[...], second[:, HD:768]).astype(BF)
        k_rot = kept[:, 2 * HD : VALUES]
        low_values = kept[:, VALUES:MIXED]
        grad_k = jnp.zeros((SEQ, HD), F32)
        grad_v = jnp.zeros((SEQ, HD), F32)
        gain = jnp.zeros((1, HD), F32)
        for head in range(2):
            at = slice(head * HD, (head + 1) * HD)
            weights = probs[head]
            back = grad_mixed[:, at]
            grad_probs = contract_cols(back, low_values)
            center = jnp.sum(weights * grad_probs, axis=-1, keepdims=True)
            grad_scores = (weights * (grad_probs - center)).astype(BF)
            grad_k = grad_k + contract_rows(grad_scores, kept[:, at])
            grad_v = grad_v + contract_rows(weights.astype(BF), back)
            grad_rot = product(grad_scores, k_rot) * SCALE
            field = kept_f[:, at]
            grad_field, terms = norm_back(
                rotate(grad_rot, cos, -sin), field, inverse_rms(field), query_scale
            )
            gain = gain + jnp.sum(terms, axis=0, keepdims=True)
            grad_q_out[:, at] = grad_field.astype(BF)
        kv_out[:, :HD] = (grad_k * SCALE).astype(BF)
        kv_out[:, HD:] = grad_v.astype(BF)
        query_gain_out[...] = jnp.broadcast_to(gain, (8, HD))
        mine = pl.multiple_of(place[1] * HALF, HALF)
        give = pl.multiple_of((1 - place[1]) * HALF, HALF)
        normed_mine[...] = contract_cols(grad_q_out[pl.ds(mine, HALF), :], first[:, : 2 * HD])
        normed_give[...] = contract_cols(grad_q_out[pl.ds(give, HALF), :], first[:, : 2 * HD]).astype(BF)

    @pl.when(place[0] == 0)
    def _():
        run(own, theirs)

    @pl.when(place[0] != 0)
    def _():
        run(theirs, own)


def input_kernel(
    place, tokens, grad_hidden, own, theirs, places, cosine, sine, gains, kept_f,
    kv_own, kv_their, part_mine, part_their, query_gain, half_gains,
    input_half, grad_kv, gain_rows,
):
    kv = kv_own[...].astype(F32) + kv_their[...].astype(F32)
    keys = kept_f[:, 2 * HD :]
    grad_keys, key_terms = norm_back(
        rotate(kv[:, :HD], cosine[...], -sine[...]), keys, inverse_rms(keys), gains[1:2, D:]
    )
    key_gain = 0.5 * jnp.sum(key_terms, axis=0, keepdims=True)
    grad_kv[:, :HD] = grad_keys.astype(BF)
    grad_kv[:, HD:] = kv[:, HD:].astype(BF)
    low = jnp.concatenate([query_gain[0:1], key_gain], axis=1)
    high = low.astype(BF)
    rest = (low - high.astype(F32)).astype(BF)

    def spread(part):
        return product(part[:, :HD], one_hot(places[0:1])) + product(part[:, HD:], one_hot(places[1:2]))

    head_row = spread(high) + spread(rest)
    mine = pl.multiple_of(place[1] * HALF, HALF)

    def run(first, second):
        grad_normed = (
            part_mine[...]
            + part_their[...].astype(F32)
            + contract_cols(grad_kv[pl.ds(mine, HALF), :HD], first[:, 2 * HD : 768])
            + contract_cols(grad_kv[pl.ds(mine, HALF), HD:], second[:, :HD])
        )
        rows = tokens[pl.ds(mine, HALF), :].astype(F32)
        add, terms = norm_back(grad_normed, rows, inverse_rms(rows), gains[0:1, :D])
        input_half[...] = grad_hidden[...] + add
        input_gain = jnp.sum(terms, axis=0, keepdims=True)
        gain_rows[...] = jnp.concatenate(
            [input_gain, half_gains[0:3], head_row, jnp.zeros((3, D), F32)], axis=0
        )

    @pl.when(place[0] == 0)
    def _():
        run(own, theirs)

    @pl.when(place[0] != 0)
    def _():
        run(theirs, own)


def weights_kernel(place, kept, grad_q, grad_kv, grad_branch, keep, give):
    normed = kept[:, MIXED + 2 * HD :]

    def run(side0, side1):
        side0[:, : 2 * HD] = contract_rows(normed, grad_q[...]).astype(BF)
        side0[:, 2 * HD :] = contract_rows(normed, grad_kv[:, :HD]).astype(BF)
        side1[:, :HD] = contract_rows(normed, grad_kv[:, HD:]).astype(BF)
        side1[:, HD:] = contract_rows(grad_branch[...], kept[:, MIXED : MIXED + 2 * HD]).astype(BF)

    @pl.when(place[0] == 0)
    def _():
        run(keep, give)

    @pl.when(place[0] != 0)
    def _():
        run(give, keep)


def assemble_kernel(keep, their, gains0, gains1, gains2, gains3, layer, out, layer_out):
    layer_out[...] = layer[...]
    out[:, :768] = (keep[...].astype(F32) + their[...].astype(F32)).astype(BF)
    sums = (gains0[...] + gains1[...]) + (gains2[...] + gains3[...])
    out[:, 768:] = contract_rows(sums.astype(BF), corner()).astype(BF)


TILES = ((0, 256), (256, 512), (512, 768), (768, 896))
ROOT = np.float32(np.sqrt(2.0 / np.pi))


def feed_kernel(*refs):
    count = len(refs) - 7
    pieces, (weights, mine, give, activ_out, gelu_out, slope_out, hold) = refs[:count], refs[count:]
    at = 0
    for piece in pieces:
        hold[at : at + piece.shape[0], :] = piece[...]
        at += piece.shape[0]
    half = at // 2
    for base, out in ((0, mine), (half, give)):
        part = slice(base, base + half)
        block = hold[part, :]
        for low, high in TILES:
            gate = product(block, weights[:, low:high])
            upper = product(block, weights[:, PAD + low : PAD + high])
            square = gate * gate
            tanh = jnp.tanh(ROOT * gate * (1.0 + 0.044715 * square))
            rise = 0.5 * (1.0 + tanh)
            gelu = gate * rise
            slope = rise + 0.5 * gate * (1.0 - tanh * tanh) * (ROOT * (1.0 + 3 * 0.044715 * square))
            gelu_out[part, low:high] = gelu.astype(BF)
            slope_out[part, low:high] = (upper * slope).astype(BF)
            activ_out[part, low:high] = (gelu * upper).astype(BF)
        out[...] = contract_cols(activ_out[part, :], weights[:, 2 * PAD :]).astype(out.dtype)


def feed_back_kernel(*refs):
    count = len(refs) - 7
    pieces, (weights, gelu, slope, mine, give, both, hold) = refs[:count], refs[count:]
    at = 0
    for piece in pieces:
        hold[at : at + piece.shape[0], :] = piece[...]
        at += piece.shape[0]
    half = at // 2
    for base, out in ((0, mine), (half, give)):
        part = slice(base, base + half)
        block = hold[part, :]
        for low, high in TILES:
            grad = product(block, weights[:, 2 * PAD + low : 2 * PAD + high])
            both[part, low:high] = (grad * slope[part, low:high].astype(F32)).astype(BF)
            both[part, PAD + low : PAD + high] = (grad * gelu[part, low:high].astype(F32)).astype(BF)
        out[...] = contract_cols(both[part, :], weights[:, : 2 * PAD]).astype(out.dtype)


def feed_weights_kernel(
    f0, f1, f2, f3, f4, f5, g0, g1, g2, g3, g4, g5, both0, both1, activ0, activ1, out, turned, right
):
    for parts, sides, start, width in (
        ((f0, f1, f2, f3, f4, f5), (both0, both1), 0, 2 * PAD),
        ((g0, g1, g2, g3, g4, g5), (activ0, activ1), 2 * PAD, PAD),
    ):
        at = 0
        for piece in parts:
            turned[:, at : at + piece.shape[0]] = piece[...].T
            at += piece.shape[0]
        right[: 2 * HALF, :width] = sides[0][...]
        right[2 * HALF :, :width] = sides[1][...]
        for low in range(0, width, 256):
            high = min(low + 256, width)
            out[:, start + low : start + high] = product(turned[...], right[:, low:high]).astype(BF)


def local(kernel, outs, count, flops, flagged=True, scratch=(), room=16):
    shapes = [jax.ShapeDtypeStruct(shape, dtype) for shape, dtype in outs]
    return pl.pallas_call(
        kernel,
        out_shape=shapes,
        in_specs=[pl.BlockSpec(memory_space=pltpu.SMEM)] * flagged
        + [pl.BlockSpec(memory_space=pltpu.VMEM)] * count,
        out_specs=[pl.BlockSpec(memory_space=pltpu.VMEM)] * len(outs),
        scratch_shapes=[pltpu.VMEM(shape, BF) for shape in scratch],
        compiler_params=pltpu.CompilerParams(vmem_limit_bytes=room * 2**20),
        cost_estimate=pl.CostEstimate(flops=flops, bytes_accessed=8 * 2**20, transcendentals=200000),
    )


def feed_forward(pieces, weights):
    rows = sum(piece.shape[0] for piece in pieces)
    units = ((rows, PAD), BF)
    return local(
        feed_kernel,
        [((rows // 2, D), F32), ((rows // 2, D), BF), units, units, units],
        len(pieces) + 1,
        rows * 6300000,
        False,
        ((rows, D),),
        24,
    )(*pieces, weights)


def feed_backward(pieces, weights, past):
    rows = sum(piece.shape[0] for piece in pieces)
    return local(
        feed_back_kernel,
        [((rows // 2, D), F32), ((rows // 2, D), BF), ((rows, 2 * PAD), BF)],
        len(pieces) + 3,
        rows * 6300000,
        False,
        ((rows, D),),
        24,
    )(*pieces, weights, past[3], past[4])


def column_cut(blocks, place):
    pieces = []
    for mask in range(4):
        block = lax.dynamic_index_in_dim(blocks, place ^ mask, 0, keepdims=False)
        pieces.append(block if mask == 0 else swap(block, ("zl", "c"), mask, 4))
    arrived = jnp.stack(pieces)
    return jnp.stack([lax.dynamic_index_in_dim(arrived, place ^ k, 0, keepdims=False) for k in range(4)])


def quarters(weight):
    cut = weight.reshape(weight.shape[0], 4, UNITS).transpose(1, 0, 2)
    return jnp.pad(cut, ((0, 0), (0, 0), (0, PAD - UNITS)))


def whole_units(block):
    return block[:, :, :UNITS].transpose(1, 0, 2).reshape(block.shape[1], 4 * UNITS)


def on_device(
    tokens,
    cotangent,
    input_gain,
    query_weight,
    key_weight,
    value_weight,
    query_gain,
    key_gain,
    output_weight,
    attention_gain,
    feed_gain,
    gate_weight,
    up_weight,
    down_weight,
    output_gain,
):
    core = lax.axis_index("c")
    member = lax.axis_index("t")
    shard = input_gain.shape[0]
    heads_gain = jnp.concatenate([query_gain, key_gain, jnp.zeros((shard - 8,), BF)])
    gains = jnp.stack([input_gain, attention_gain, feed_gain, output_gain, heads_gain], axis=1)
    gains = jnp.pad(gains, ((0, 0), (0, 123)))
    half0 = jnp.concatenate([query_weight, key_weight, gains], axis=1)
    half1 = jnp.concatenate([value_weight, output_weight.T, gains], axis=1)
    column = 2 * lax.axis_index("zl") + core
    pack = jnp.concatenate(
        [
            jnp.stack([half0, half1, half0, half1]),
            quarters(gate_weight),
            quarters(up_weight),
            quarters(down_weight.T),
        ],
        axis=2,
    )
    shards = column_cut(pack, column).reshape(4 * shard, 4 * PAD)
    att_shard, ffn_shard = shards[:, :PAD], shards[:, PAD:]
    att_half = lax.all_to_all(
        jnp.broadcast_to(att_shard[None], (16, *att_shard.shape)), PLANE, 0, 0, tiled=True
    ).reshape(D, PAD)
    feed_weights = lax.all_gather(ffn_shard, PLANE, axis=0, tiled=True)

    flag = jnp.stack([core, member]).astype(jnp.int32)
    their_half = other_core(att_half)
    cosine, sine = tables()
    places = head_places()
    gains, kept, kept_f, probs_f, branch_mine, branch_give = local(
        attend_kernel,
        [
            ((8, D + HD), F32), ((SEQ, MIXED + 2 * HD + D), BF), ((SEQ, 768), F32), ((2, SEQ, SEQ), F32),
            ((HALF, D), F32), ((HALF, D), BF),
        ],
        6,
        1100000000,
        room=60,
    )(flag, tokens, att_half, their_half, places, cosine, sine)
    post_gain, feed_scale, final_gain = (gains[i : i + 1, :D] for i in (1, 2, 3))

    def my_half(field):
        return lax.dynamic_slice_in_dim(field, member * HALF, HALF, 0)

    def whole_rows(field, theirs):
        top = jnp.where(member == 0, field, theirs)
        bottom = jnp.where(member == 0, theirs, field)
        return jnp.concatenate([top, bottom], axis=0)

    branch = branch_mine + other_member(branch_give).astype(F32)
    my_rows = my_half(tokens).astype(F32)
    inv_b = inverse_rms(branch)
    hidden = my_rows + branch * inv_b * post_gain
    inv_h = inverse_rms(hidden)
    feed = (hidden * inv_h * feed_scale).astype(BF)

    feeds, saved = near_and_far(feed, lambda _, pieces: feed_forward(pieces, feed_weights))
    second = summed(saved[0], core_sum(saved[1]))
    inv_s = inverse_rms(second)
    layer_half = (hidden + second * inv_s * final_gain).astype(BF)

    upstream = my_half(cotangent).astype(F32)
    grad_second, final_terms = norm_back(upstream, second, inv_s, final_gain)
    grads, backs = near_and_far(
        grad_second.astype(BF), lambda i, pieces: feed_backward(pieces, feed_weights, saved[i])
    )
    feed_back = summed(backs[0], core_sum(backs[1]))
    (ffn_grads,) = local(
        feed_weights_kernel,
        [((D, 3 * PAD), BF)],
        16,
        6300000000,
        False,
        ((D, 8 * HALF), (8 * HALF, 2 * PAD)),
        30,
    )(*feeds, *grads, backs[0][2], backs[1][2], saved[0][2], saved[1][2])
    ffn_sums = lax.psum_scatter(ffn_grads, PLANE, scatter_dimension=0, tiled=True)
    hidden_add, feed_terms = norm_back(feed_back, hidden, inv_h, feed_scale)
    grad_hidden = upstream + hidden_add
    grad_branch, post_terms = norm_back(grad_hidden, branch, inv_b, post_gain)
    grad_mine = grad_branch.astype(BF)
    half_gains = jnp.stack([jnp.sum(terms, axis=0) for terms in (post_terms, feed_terms, final_terms)])
    half_gains = jnp.pad(half_gains, ((0, 5), (0, 0)))

    grad_branch, kv_part, grad_q, normed_mine, normed_give, query_gain = local(
        attend_back_kernel,
        [
            ((SEQ, D), BF), ((SEQ, 2 * HD), BF), ((SEQ, 2 * HD), BF), ((HALF, D), F32), ((HALF, D), BF),
            ((8, HD), F32),
        ],
        10,
        1100000000,
    )(flag, grad_mine, other_member(grad_mine), att_half, their_half, cosine, sine, gains, kept, kept_f, probs_f)
    input_half, grad_kv, gain_rows = local(
        input_kernel,
        [((HALF, D), F32), ((SEQ, 2 * HD), BF), ((8, D), F32)],
        15,
        400000000,
    )(
        flag, tokens, grad_hidden, att_half, their_half, places, cosine, sine, gains, kept_f,
        kv_part, other_member(kv_part), normed_mine, other_member(normed_give), query_gain, half_gains,
    )
    keep, give = local(weights_kernel, [((D, 768), BF), ((D, 768), BF)], 4, 900000000)(
        flag, kept, grad_q, grad_kv, grad_branch
    )
    att_sums, layer_half = local(
        assemble_kernel, [((D, PAD), BF), ((HALF, D), BF)], 7, 10000000, False
    )(
        keep,
        other_core(give),
        gain_rows,
        *(swap(gain_rows, ("c", "t"), mask, 4) for mask in (2, 1, 3)),
        layer_half,
    )
    att_sums, input_half = lax.optimization_barrier((att_sums, input_half))
    ffn_sums = column_cut(ffn_sums.reshape(4, shard, 3 * PAD), column)
    input_grad = whole_rows(input_half, other_member(input_half))
    layer_out = whole_rows(layer_half, other_member(layer_half))
    att_sums = lax.all_to_all(att_sums.reshape(16, 4 * shard, PAD), PLANE, 0, 0, tiled=True)
    att_sums = jnp.sum(att_sums.astype(F32), axis=0).astype(BF)
    att_sums, ffn_sums = lax.optimization_barrier((att_sums, ffn_sums))
    ffn_sums = ffn_sums.astype(F32)
    grad_gate_weight = whole_units(ffn_sums[:, :, :PAD])
    grad_up_weight = whole_units(ffn_sums[:, :, PAD : 2 * PAD])
    grad_down = whole_units(ffn_sums[:, :, 2 * PAD :]).T
    att_sums = lax.all_to_all(att_sums.reshape(4, shard, PAD), ("zl", "c"), 0, 0, tiled=True).astype(F32)
    out0 = att_sums[0] + att_sums[2]
    out1 = att_sums[1] + att_sums[3]

    return (
        layer_out,
        input_grad,
        out0[:, 768],
        out0[:, :512],
        out0[:, 512:768],
        out1[:, :256],
        out0[:4, 772],
        out0[4:8, 772],
        out1[:, 256:768].T,
        out0[:, 769],
        out0[:, 770],
        grad_gate_weight,
        grad_up_weight,
        grad_down,
        out0[:, 771],
    )


def solution(mesh):
    fine = Mesh(mesh.devices.reshape(4, 4, 2, 2, 2), ("y", "x", "zl", "c", "t"))
    dp = ("y", "x", "zl", "c")
    in_specs = (
        P(dp, None),
        P(dp, None),
        P(dp),
        P(dp, "t"),
        P(dp, None),
        P(dp, None),
        P(dp),
        P(dp),
        P("t", dp),
        P(dp),
        P(dp),
        P(dp, "t"),
        P(dp, "t"),
        P("t", dp),
        P(dp),
    )
    out_specs = (
        P(dp, None),
        P(dp, None),
        P(dp),
        P(dp, "t"),
        P(dp, None),
        P(dp, None),
        P(dp),
        P(dp),
        P("t", dp),
        P(dp),
        P(dp),
        P(dp, "t"),
        P(dp, "t"),
        P("t", dp),
        P(dp),
    )
    return jax.shard_map(
        on_device, mesh=fine, in_specs=in_specs, out_specs=out_specs, check_vma=False
    )
```

```python
import jax
import jax.numpy as jnp
import numpy as np
from jax import lax
from jax.experimental import pallas as pl
from jax.experimental.pallas import tpu as pltpu
from jax.sharding import Mesh, PartitionSpec as P

D = 1152
HD = 256
SEQ = 256
HALF = SEQ // 2
UNITS = 864
VALUES = 768
MIXED = 1024
PAD = 896
EPS = 1e-06
THETA = 1000000.0
SCALE = HD ** (-0.5)
BF = jnp.bfloat16
F32 = jnp.float32
PLANE = ("y", "x")


def swap(field, axes, mask, size):
    return lax.ppermute(field, axes, [(i, i ^ mask) for i in range(size)])


def across(field, mask):
    return swap(field, ("zl", "t"), mask, 4)


def other_core(field):
    return swap(field, "c", 1, 2)


def other_member(field):
    return swap(field, "t", 1, 2)


def near_and_far(block, run):
    near = (block, other_core(block))
    far = [across(block, m) for m in (1, 2, 3)]
    first, *rest = run(0, near)
    first, *far = lax.optimization_barrier((first, *far))
    far = (*far, other_core(jnp.concatenate(far, axis=0)))
    return (*near, *far), [(first, *rest), run(1, far)]


def core_sum(far):
    return (far[0] + other_core(far[1]).astype(F32)).astype(BF)


def summed(near, mine):
    far = [across(mine[(m - 1) * HALF : m * HALF], m) for m in (1, 2, 3)]
    total = near[0] + other_core(near[1]).astype(F32)
    for field in far:
        total = total + field.astype(F32)
    return total


def product(left, right):
    return jnp.dot(left, right, preferred_element_type=F32)


def contract_rows(left, right):
    return lax.dot_general(left, right, (((0,), (0,)), ((), ())), preferred_element_type=F32)


def contract_cols(left, right):
    return lax.dot_general(left, right, (((1,), (1,)), ((), ())), preferred_element_type=F32)


def inverse_rms(field):
    return lax.rsqrt(jnp.mean(field * field, axis=-1, keepdims=True) + EPS)


def norm_back(grad, field, inv, gain):
    scaled = grad * gain
    back = inv * scaled - field * (inv * inv * inv) * jnp.mean(field * scaled, axis=-1, keepdims=True)
    return back, grad * field * inv


def tables():
    half = HD // 2
    freq = np.float32(THETA) ** (-np.arange(half, dtype=np.float32) / np.float32(half))
    angle = np.arange(SEQ, dtype=np.float32)[:, None] * freq[None, :].astype(np.float32)
    return jnp.asarray(np.cos(angle).astype(np.float32)), jnp.asarray(np.sin(angle).astype(np.float32))


def rotate(field, cosine, sine):
    half = HD // 2
    first, second = field[..., :half], field[..., half:]
    return jnp.concatenate([first * cosine - second * sine, second * cosine + first * sine], axis=-1)


def head_places():
    place = np.full((2, D), -1, np.int32)
    for row in range(D):
        group, at = divmod(row, 18)
        if at < 8:
            place[at // 4, row] = 4 * group + at % 4
    return jnp.asarray(np.concatenate([place, np.zeros((6, D), np.int32)]))


def one_hot(place_row):
    rows = lax.broadcasted_iota(jnp.int32, (HD, D), 0)
    return jnp.where(rows == place_row, 1.0, 0.0).astype(BF)


def corner():
    rows = lax.broadcasted_iota(jnp.int32, (8, 128), 0)
    return jnp.where(rows == lax.broadcasted_iota(jnp.int32, (8, 128), 1), 1.0, 0.0).astype(BF)


def attend_kernel(
    place, tokens, own, theirs, places, cosine, sine,
    gains, kept, kept_f, probs_out, branch_mine, branch_give,
):
    all_gains = contract_cols(corner(), own[:, 768:])
    head_row = all_gains[4:5].astype(BF)
    query_scale = contract_cols(head_row, one_hot(places[0:1]))
    key_scale = contract_cols(head_row, one_hot(places[1:2]))
    gains[:, :D] = all_gains
    gains[:, D:] = jnp.concatenate([query_scale, key_scale, jnp.zeros((6, HD), F32)], axis=0)
    rows = tokens[...].astype(F32)
    normed = (rows * inverse_rms(rows) * all_gains[0:1]).astype(BF)
    kept[:, MIXED + 2 * HD :] = normed

    def run(first, second):
        cos, sin = cosine[...], sine[...]
        qk = product(normed, first[:, :768])
        kept_f[...] = qk
        values = product(normed, second[:, :HD]).astype(BF)
        kept[:, VALUES:MIXED] = values

        def prepare(field, scale):
            return rotate(field * inverse_rms(field) * scale, cos, sin).astype(BF)

        k_rot = prepare(qk[:, 2 * HD :], key_scale)
        kept[:, 2 * HD : VALUES] = k_rot
        causal = lax.broadcasted_iota(jnp.int32, (SEQ, SEQ), 1) <= lax.broadcasted_iota(
            jnp.int32, (SEQ, SEQ), 0
        )
        for head in range(2):
            at = slice(head * HD, (head + 1) * HD)
            q_rot = prepare(qk[:, at], query_scale)
            kept[:, at] = q_rot
            scores = jnp.where(causal, contract_cols(q_rot, k_rot) * SCALE, -1e30)
            expo = jnp.exp(scores - jnp.max(scores, axis=-1, keepdims=True))
            probs = expo / jnp.sum(expo, axis=-1, keepdims=True)
            probs_out[head] = probs
            kept[:, MIXED + head * HD : MIXED + (head + 1) * HD] = product(probs.astype(BF), values).astype(BF)
        mine = pl.multiple_of(place[1] * HALF, HALF)
        give = pl.multiple_of((1 - place[1]) * HALF, HALF)
        mixed = MIXED + 2 * HD
        branch_mine[...] = contract_cols(kept[pl.ds(mine, HALF), MIXED:mixed], second[:, HD:768])
        branch_give[...] = contract_cols(kept[pl.ds(give, HALF), MIXED:mixed], second[:, HD:768]).astype(BF)

    @pl.when(place[0] == 0)
    def _():
        run(own, theirs)

    @pl.when(place[0] != 0)
    def _():
        run(theirs, own)


def attend_back_kernel(
    place, grad_mine, grad_their, own, theirs, cosine, sine, gains, kept, kept_f, probs,
    grad, kv_out, grad_q_out, normed_mine, normed_give, query_gain_out,
):
    grad[pl.ds(pl.multiple_of(place[1] * HALF, HALF), HALF), :] = grad_mine[...]
    grad[pl.ds(pl.multiple_of((1 - place[1]) * HALF, HALF), HALF), :] = grad_their[...]

    def run(first, second):
        cos, sin = cosine[...], sine[...]
        query_scale = gains[0:1, D:]
        grad_mixed = product(grad[...], second[:, HD:768]).astype(BF)
        k_rot = kept[:, 2 * HD : VALUES]
        low_values = kept[:, VALUES:MIXED]
        grad_k = jnp.zeros((SEQ, HD), F32)
        grad_v = jnp.zeros((SEQ, HD), F32)
        gain = jnp.zeros((1, HD), F32)
        for head in range(2):
            at = slice(head * HD, (head + 1) * HD)
            weights = probs[head]
            back = grad_mixed[:, at]
            grad_probs = contract_cols(back, low_values)
            center = jnp.sum(weights * grad_probs, axis=-1, keepdims=True)
            grad_scores = (weights * (grad_probs - center)).astype(BF)
            grad_k = grad_k + contract_rows(grad_scores, kept[:, at])
            grad_v = grad_v + contract_rows(weights.astype(BF), back)
            grad_rot = product(grad_scores, k_rot) * SCALE
            field = kept_f[:, at]
            grad_field, terms = norm_back(
                rotate(grad_rot, cos, -sin), field, inverse_rms(field), query_scale
            )
            gain = gain + jnp.sum(terms, axis=0, keepdims=True)
            grad_q_out[:, at] = grad_field.astype(BF)
        kv_out[:, :HD] = (grad_k * SCALE).astype(BF)
        kv_out[:, HD:] = grad_v.astype(BF)
        query_gain_out[...] = jnp.broadcast_to(gain, (8, HD))
        mine = pl.multiple_of(place[1] * HALF, HALF)
        give = pl.multiple_of((1 - place[1]) * HALF, HALF)
        normed_mine[...] = contract_cols(grad_q_out[pl.ds(mine, HALF), :], first[:, : 2 * HD])
        normed_give[...] = contract_cols(grad_q_out[pl.ds(give, HALF), :], first[:, : 2 * HD]).astype(BF)

    @pl.when(place[0] == 0)
    def _():
        run(own, theirs)

    @pl.when(place[0] != 0)
    def _():
        run(theirs, own)


def input_kernel(
    place, tokens, grad_hidden, own, theirs, places, cosine, sine, gains, kept_f,
    kv_own, kv_their, part_mine, part_their, query_gain, half_gains,
    input_half, grad_kv, gain_rows,
):
    kv = kv_own[...].astype(F32) + kv_their[...].astype(F32)
    keys = kept_f[:, 2 * HD :]
    grad_keys, key_terms = norm_back(
        rotate(kv[:, :HD], cosine[...], -sine[...]), keys, inverse_rms(keys), gains[1:2, D:]
    )
    key_gain = 0.5 * jnp.sum(key_terms, axis=0, keepdims=True)
    grad_kv[:, :HD] = grad_keys.astype(BF)
    grad_kv[:, HD:] = kv[:, HD:].astype(BF)
    low = jnp.concatenate([query_gain[0:1], key_gain], axis=1)
    high = low.astype(BF)
    rest = (low - high.astype(F32)).astype(BF)

    def spread(part):
        return product(part[:, :HD], one_hot(places[0:1])) + product(part[:, HD:], one_hot(places[1:2]))

    head_row = spread(high) + spread(rest)
    mine = pl.multiple_of(place[1] * HALF, HALF)

    def run(first, second):
        grad_normed = (
            part_mine[...]
            + part_their[...].astype(F32)
            + contract_cols(grad_kv[pl.ds(mine, HALF), :HD], first[:, 2 * HD : 768])
            + contract_cols(grad_kv[pl.ds(mine, HALF), HD:], second[:, :HD])
        )
        rows = tokens[pl.ds(mine, HALF), :].astype(F32)
        add, terms = norm_back(grad_normed, rows, inverse_rms(rows), gains[0:1, :D])
        input_half[...] = grad_hidden[...] + add
        input_gain = jnp.sum(terms, axis=0, keepdims=True)
        gain_rows[...] = jnp.concatenate(
            [input_gain, half_gains[0:3], head_row, jnp.zeros((3, D), F32)], axis=0
        )

    @pl.when(place[0] == 0)
    def _():
        run(own, theirs)

    @pl.when(place[0] != 0)
    def _():
        run(theirs, own)


def weights_kernel(place, kept, grad_q, grad_kv, grad_branch, keep, give):
    normed = kept[:, MIXED + 2 * HD :]

    def run(side0, side1):
        side0[:, : 2 * HD] = contract_rows(normed, grad_q[...]).astype(BF)
        side0[:, 2 * HD :] = contract_rows(normed, grad_kv[:, :HD]).astype(BF)
        side1[:, :HD] = contract_rows(normed, grad_kv[:, HD:]).astype(BF)
        side1[:, HD:] = contract_rows(grad_branch[...], kept[:, MIXED : MIXED + 2 * HD]).astype(BF)

    @pl.when(place[0] == 0)
    def _():
        run(keep, give)

    @pl.when(place[0] != 0)
    def _():
        run(give, keep)


def assemble_kernel(keep, their, gains0, gains1, gains2, gains3, layer, out, layer_out):
    layer_out[...] = layer[...]
    out[:, :768] = (keep[...].astype(F32) + their[...].astype(F32)).astype(BF)
    sums = (gains0[...] + gains1[...]) + (gains2[...] + gains3[...])
    out[:, 768:] = contract_rows(sums.astype(BF), corner()).astype(BF)


TILES = ((0, 256), (256, 512), (512, 768), (768, 896))
ROOT = np.float32(np.sqrt(2.0 / np.pi))


def feed_kernel(*refs):
    count = len(refs) - 7
    pieces, (weights, mine, give, activ_out, gelu_out, slope_out, hold) = refs[:count], refs[count:]
    at = 0
    for piece in pieces:
        hold[at : at + piece.shape[0], :] = piece[...]
        at += piece.shape[0]
    half = at // 2
    for base, out in ((0, mine), (half, give)):
        part = slice(base, base + half)
        block = hold[part, :]
        for low, high in TILES:
            gate = product(block, weights[:, low:high])
            upper = product(block, weights[:, PAD + low : PAD + high])
            square = gate * gate
            tanh = jnp.tanh(ROOT * gate * (1.0 + 0.044715 * square))
            rise = 0.5 * (1.0 + tanh)
            gelu = gate * rise
            slope = rise + 0.5 * gate * (1.0 - tanh * tanh) * (ROOT * (1.0 + 3 * 0.044715 * square))
            gelu_out[part, low:high] = gelu.astype(BF)
            slope_out[part, low:high] = (upper * slope).astype(BF)
            activ_out[part, low:high] = (gelu * upper).astype(BF)
        out[...] = contract_cols(activ_out[part, :], weights[:, 2 * PAD :]).astype(out.dtype)


def feed_back_kernel(*refs):
    count = len(refs) - 7
    pieces, (weights, gelu, slope, mine, give, both, hold) = refs[:count], refs[count:]
    at = 0
    for piece in pieces:
        hold[at : at + piece.shape[0], :] = piece[...]
        at += piece.shape[0]
    half = at // 2
    for base, out in ((0, mine), (half, give)):
        part = slice(base, base + half)
        block = hold[part, :]
        for low, high in TILES:
            grad = product(block, weights[:, 2 * PAD + low : 2 * PAD + high])
            both[part, low:high] = (grad * slope[part, low:high].astype(F32)).astype(BF)
            both[part, PAD + low : PAD + high] = (grad * gelu[part, low:high].astype(F32)).astype(BF)
        out[...] = contract_cols(both[part, :], weights[:, : 2 * PAD]).astype(out.dtype)


def feed_weights_kernel(
    f0, f1, f2, f3, f4, f5, g0, g1, g2, g3, g4, g5, both0, both1, activ0, activ1, out, turned, right
):
    for parts, sides, start, width in (
        ((f0, f1, f2, f3, f4, f5), (both0, both1), 0, 2 * PAD),
        ((g0, g1, g2, g3, g4, g5), (activ0, activ1), 2 * PAD, PAD),
    ):
        at = 0
        for piece in parts:
            turned[:, at : at + piece.shape[0]] = piece[...].T
            at += piece.shape[0]
        right[: 2 * HALF, :width] = sides[0][...]
        right[2 * HALF :, :width] = sides[1][...]
        for low in range(0, width, 256):
            high = min(low + 256, width)
            out[:, start + low : start + high] = product(turned[...], right[:, low:high]).astype(BF)


def local(kernel, outs, count, flops, flagged=True, scratch=(), room=16):
    shapes = [jax.ShapeDtypeStruct(shape, dtype) for shape, dtype in outs]
    return pl.pallas_call(
        kernel,
        out_shape=shapes,
        in_specs=[pl.BlockSpec(memory_space=pltpu.SMEM)] * flagged
        + [pl.BlockSpec(memory_space=pltpu.VMEM)] * count,
        out_specs=[pl.BlockSpec(memory_space=pltpu.VMEM)] * len(outs),
        scratch_shapes=[pltpu.VMEM(shape, BF) for shape in scratch],
        compiler_params=pltpu.CompilerParams(vmem_limit_bytes=room * 2**20),
        cost_estimate=pl.CostEstimate(flops=flops, bytes_accessed=8 * 2**20, transcendentals=200000),
    )


def feed_forward(pieces, weights):
    rows = sum(piece.shape[0] for piece in pieces)
    units = ((rows, PAD), BF)
    return local(
        feed_kernel,
        [((rows // 2, D), F32), ((rows // 2, D), BF), units, units, units],
        len(pieces) + 1,
        rows * 6300000,
        False,
        ((rows, D),),
        24,
    )(*pieces, weights)


def feed_backward(pieces, weights, past):
    rows = sum(piece.shape[0] for piece in pieces)
    return local(
        feed_back_kernel,
        [((rows // 2, D), F32), ((rows // 2, D), BF), ((rows, 2 * PAD), BF)],
        len(pieces) + 3,
        rows * 6300000,
        False,
        ((rows, D),),
        24,
    )(*pieces, weights, past[3], past[4])


def column_cut(blocks, place):
    pieces = []
    for mask in range(4):
        block = lax.dynamic_index_in_dim(blocks, place ^ mask, 0, keepdims=False)
        pieces.append(block if mask == 0 else swap(block, ("zl", "c"), mask, 4))
    arrived = jnp.stack(pieces)
    return jnp.stack([lax.dynamic_index_in_dim(arrived, place ^ k, 0, keepdims=False) for k in range(4)])


def quarters(weight):
    cut = weight.reshape(weight.shape[0], 4, UNITS).transpose(1, 0, 2)
    return jnp.pad(cut, ((0, 0), (0, 0), (0, PAD - UNITS)))


def whole_units(block):
    return block[:, :, :UNITS].transpose(1, 0, 2).reshape(block.shape[1], 4 * UNITS)


def on_device(
    tokens,
    cotangent,
    input_gain,
    query_weight,
    key_weight,
    value_weight,
    query_gain,
    key_gain,
    output_weight,
    attention_gain,
    feed_gain,
    gate_weight,
    up_weight,
    down_weight,
    output_gain,
):
    core = lax.axis_index("c")
    member = lax.axis_index("t")
    shard = input_gain.shape[0]
    heads_gain = jnp.concatenate([query_gain, key_gain, jnp.zeros((shard - 8,), BF)])
    gains = jnp.stack([input_gain, attention_gain, feed_gain, output_gain, heads_gain], axis=1)
    gains = jnp.pad(gains, ((0, 0), (0, 123)))
    half0 = jnp.concatenate([query_weight, key_weight, gains], axis=1)
    half1 = jnp.concatenate([value_weight, output_weight.T, gains], axis=1)
    column = 2 * lax.axis_index("zl") + core
    pack = jnp.concatenate(
        [
            jnp.stack([half0, half1, half0, half1]),
            quarters(gate_weight),
            quarters(up_weight),
            quarters(down_weight.T),
        ],
        axis=2,
    )
    shards = column_cut(pack, column).reshape(4 * shard, 4 * PAD)
    att_shard, ffn_shard = shards[:, :PAD], shards[:, PAD:]
    att_half = lax.all_to_all(
        jnp.broadcast_to(att_shard[None], (16, *att_shard.shape)), PLANE, 0, 0, tiled=True
    ).reshape(D, PAD)
    feed_weights = lax.all_gather(ffn_shard, PLANE, axis=0, tiled=True)

    flag = jnp.stack([core, member]).astype(jnp.int32)
    their_half = other_core(att_half)
    cosine, sine = tables()
    places = head_places()
    gains, kept, kept_f, probs_f, branch_mine, branch_give = local(
        attend_kernel,
        [
            ((8, D + HD), F32), ((SEQ, MIXED + 2 * HD + D), BF), ((SEQ, 768), F32), ((2, SEQ, SEQ), F32),
            ((HALF, D), F32), ((HALF, D), BF),
        ],
        6,
        1100000000,
        room=60,
    )(flag, tokens, att_half, their_half, places, cosine, sine)
    post_gain, feed_scale, final_gain = (gains[i : i + 1, :D] for i in (1, 2, 3))

    def my_half(field):
        return lax.dynamic_slice_in_dim(field, member * HALF, HALF, 0)

    def whole_rows(field, theirs):
        top = jnp.where(member == 0, field, theirs)
        bottom = jnp.where(member == 0, theirs, field)
        return jnp.concatenate([top, bottom], axis=0)

    branch = branch_mine + other_member(branch_give).astype(F32)
    my_rows = my_half(tokens).astype(F32)
    inv_b = inverse_rms(branch)
    hidden = my_rows + branch * inv_b * post_gain
    inv_h = inverse_rms(hidden)
    feed = (hidden * inv_h * feed_scale).astype(BF)

    feeds, saved = near_and_far(feed, lambda _, pieces: feed_forward(pieces, feed_weights))
    second = summed(saved[0], core_sum(saved[1]))
    inv_s = inverse_rms(second)
    layer_half = (hidden + second * inv_s * final_gain).astype(BF)

    upstream = my_half(cotangent).astype(F32)
    grad_second, final_terms = norm_back(upstream, second, inv_s, final_gain)
    grads, backs = near_and_far(
        grad_second.astype(BF), lambda i, pieces: feed_backward(pieces, feed_weights, saved[i])
    )
    feed_back = summed(backs[0], core_sum(backs[1]))
    (ffn_grads,) = local(
        feed_weights_kernel,
        [((D, 3 * PAD), BF)],
        16,
        6300000000,
        False,
        ((D, 8 * HALF), (8 * HALF, 2 * PAD)),
        30,
    )(*feeds, *grads, backs[0][2], backs[1][2], saved[0][2], saved[1][2])
    ffn_sums = lax.psum_scatter(ffn_grads, PLANE, scatter_dimension=0, tiled=True)
    hidden_add, feed_terms = norm_back(feed_back, hidden, inv_h, feed_scale)
    grad_hidden = upstream + hidden_add
    grad_branch, post_terms = norm_back(grad_hidden, branch, inv_b, post_gain)
    grad_mine = grad_branch.astype(BF)
    half_gains = jnp.stack([jnp.sum(terms, axis=0) for terms in (post_terms, feed_terms, final_terms)])
    half_gains = jnp.pad(half_gains, ((0, 5), (0, 0)))

    grad_branch, kv_part, grad_q, normed_mine, normed_give, query_gain = local(
        attend_back_kernel,
        [
            ((SEQ, D), BF), ((SEQ, 2 * HD), BF), ((SEQ, 2 * HD), BF), ((HALF, D), F32), ((HALF, D), BF),
            ((8, HD), F32),
        ],
        10,
        1100000000,
    )(flag, grad_mine, other_member(grad_mine), att_half, their_half, cosine, sine, gains, kept, kept_f, probs_f)
    input_half, grad_kv, gain_rows = local(
        input_kernel,
        [((HALF, D), F32), ((SEQ, 2 * HD), BF), ((8, D), F32)],
        15,
        400000000,
    )(
        flag, tokens, grad_hidden, att_half, their_half, places, cosine, sine, gains, kept_f,
        kv_part, other_member(kv_part), normed_mine, other_member(normed_give), query_gain, half_gains,
    )
    keep, give = local(weights_kernel, [((D, 768), BF), ((D, 768), BF)], 4, 900000000)(
        flag, kept, grad_q, grad_kv, grad_branch
    )
    att_sums, layer_half = local(
        assemble_kernel, [((D, PAD), BF), ((HALF, D), BF)], 7, 10000000, False
    )(
        keep,
        other_core(give),
        gain_rows,
        *(swap(gain_rows, ("c", "t"), mask, 4) for mask in (2, 1, 3)),
        layer_half,
    )
    att_sums, input_half = lax.optimization_barrier((att_sums, input_half))
    input_grad = whole_rows(input_half, other_member(input_half))
    layer_out = whole_rows(layer_half, other_member(layer_half))
    att_sums = lax.all_to_all(att_sums.reshape(16, 4 * shard, PAD), PLANE, 0, 0, tiled=True)
    att_sums = jnp.sum(att_sums.astype(F32), axis=0).astype(BF)
    both_sums = jnp.concatenate(
        [att_sums.reshape(4, shard, PAD), ffn_sums.reshape(4, shard, 3 * PAD)], axis=2
    )
    both_sums = column_cut(both_sums, column).astype(F32)
    att_sums, ffn_sums = both_sums[:, :, :PAD], both_sums[:, :, PAD:]
    grad_gate_weight = whole_units(ffn_sums[:, :, :PAD])
    grad_up_weight = whole_units(ffn_sums[:, :, PAD : 2 * PAD])
    grad_down = whole_units(ffn_sums[:, :, 2 * PAD :]).T
    out0 = att_sums[0] + att_sums[2]
    out1 = att_sums[1] + att_sums[3]

    return (
        layer_out,
        input_grad,
        out0[:, 768],
        out0[:, :512],
        out0[:, 512:768],
        out1[:, :256],
        out0[:4, 772],
        out0[4:8, 772],
        out1[:, 256:768].T,
        out0[:, 769],
        out0[:, 770],
        grad_gate_weight,
        grad_up_weight,
        grad_down,
        out0[:, 771],
    )


def solution(mesh):
    fine = Mesh(mesh.devices.reshape(4, 4, 2, 2, 2), ("y", "x", "zl", "c", "t"))
    dp = ("y", "x", "zl", "c")
    in_specs = (
        P(dp, None),
        P(dp, None),
        P(dp),
        P(dp, "t"),
        P(dp, None),
        P(dp, None),
        P(dp),
        P(dp),
        P("t", dp),
        P(dp),
        P(dp),
        P(dp, "t"),
        P(dp, "t"),
        P("t", dp),
        P(dp),
    )
    out_specs = (
        P(dp, None),
        P(dp, None),
        P(dp),
        P(dp, "t"),
        P(dp, None),
        P(dp, None),
        P(dp),
        P(dp),
        P("t", dp),
        P(dp),
        P(dp),
        P(dp, "t"),
        P(dp, "t"),
        P("t", dp),
        P(dp),
    )
    return jax.shard_map(
        on_device, mesh=fine, in_specs=in_specs, out_specs=out_specs, check_vma=False
    )
```
